128 devices in a mesh: row: 8 (over y, core), col: 16 (over x, z).
Axes of the slice: x: 4, y: 4, z: 4, core: 2. Of those that a mesh axis runs over, the one named last changes fastest.
Arguments:
- densities: bfloat16 [2, 256, 12288], P(None, 'row', 'col'), may hold values from -6 to 6
- pair_weight: bfloat16 [256], P('row'), may hold values from 0.099609375 to 1
- block_perm: int32 [8, 96], replicated, may hold values from 0 to 95, as said below
- phase_index: int32 [8, 12288], replicated, may hold values from 0 to 7
Outputs:
- chi_sym: float32 [2, 12288, 12288], P(None, 'row', 'col')
The draws below stay inside these ranges and needn't reach their ends.
Inputs may be any that keep to these rules, and one draw needn't show every extreme that they name: `block_perm`: each row is a permutation of the 96 blocks that maps every aligned group of 12 consecutive blocks onto itself.
All inputs are finite; a program needn't handle non-finite values.
Results may differ from the reference program's by a relative error of at most 0.0033.
Values may be sent and summed in bfloat16 or wider, within the bound.
A program may use at most 192 MiB of HBM per device.

```python
import math
import jax
import jax.numpy as jnp
from jax import lax

NG = 12288
BLOCK = 128
NS = 8
ORDER = 8
PAIRS = 256
NB = 96
GROUP = 12


def draw_block_perm(key, part):
    key = jax.random.fold_in(key, 11)
    groups = NB // GROUP
    keys = jax.random.split(key, NS * groups)
    shuffled = jax.vmap(lambda single: jax.random.permutation(single, GROUP))(keys)
    shuffled = shuffled.reshape(NS, groups, GROUP).astype(jnp.int32)
    offsets = (jnp.arange(groups, dtype=jnp.int32) * GROUP)[None, :, None]
    return (shuffled + offsets).reshape(NS, NB).astype(jnp.int32)


def place_ends(drawn, own_key, low, top_value):
    dims = drawn.shape
    index_at = [jax.random.randint(jax.random.fold_in(own_key, axis), (), 0, dims[axis]) for axis in range(len(dims))]
    drawn = drawn.at[tuple(index_at)].set(low)
    longest = dims.index(max(dims))
    index_at[longest] = (index_at[longest] + 1) % dims[longest]
    return drawn.at[tuple(index_at)].set(top_value)


def steps_of(own_key, dims, cuts, least, top_value):
    loudness, own = 1.0, jax.random.fold_in(own_key, 6)
    for position, shards_of in cuts:
        draws = jnp.exp(jax.random.uniform(jax.random.fold_in(own, position), (shards_of,), jnp.float32, least / len(cuts), top_value / len(cuts)))
        loudness = loudness * jnp.repeat(draws, dims[position] // shards_of).reshape([-1 if axis == position else 1 for axis in range(len(dims))])
    return loudness


def bell_draw(rng, dims, width, reach, cuts=(), held_as=jnp.bfloat16):
    factor_of = steps_of(rng, dims, cuts, -0.22, 0.18) if cuts else 1.0
    entries = jax.random.normal(rng, dims, jnp.float32) * width * factor_of
    return jnp.minimum(jnp.maximum(entries, -reach), reach).astype(held_as)


def setup_inputs(seed: int = 0) -> dict:
    splits = jax.random.split(jax.random.key(seed), 5)
    return {
        "densities": bell_draw(splits[0], (2, PAIRS, NG), 1.0, 6.0, ((1, 8), (2, 16))),
        "pair_weight": jnp.clip(jnp.exp(math.log(1.0) - 2.306499 * jax.random.uniform(splits[1], (PAIRS,), jnp.float32) ** steps_of(splits[1], (PAIRS,), ((0, 8),), -0.2, 0.2)), 0.099609375, 1.0).astype(jnp.bfloat16),
        "block_perm": draw_block_perm(jax.random.fold_in(splits[4], 71), 0),
        "phase_index": place_ends(jax.random.randint(splits[3], (NS, NG), 0, ORDER), jax.random.fold_in(splits[3], 1), 0, ORDER - 1).astype(jnp.int32),
    }


full_turn = 2.0 * math.pi

def rotate_all(densities, order_row, phase_row):
    index = (order_row[:, None] * BLOCK + jnp.arange(BLOCK, dtype=jnp.int32)[None, :]).reshape(-1).astype(jnp.int32)
    picked = jnp.take(densities, index, axis=2).astype(jnp.float32)
    angles = phase_row.astype(jnp.float32) * (full_turn / ORDER)
    cosine = jnp.cos(angles)
    sine_value = jnp.sin(angles)
    rotated_real = cosine * picked[0] - sine_value * picked[1]
    rotated_imag = sine_value * picked[0] + cosine * picked[1]
    return (rotated_real, rotated_imag)

def reference(densities, pair_weight, block_perm, phase_index):
    weight_col = pair_weight.astype(jnp.float32)[:, None]
    accumulated = jnp.zeros((NG, 2 * NG), jnp.float32)
    for operation in range(NS):
        rotated_real, rotated_imag = rotate_all(densities, block_perm[operation], phase_index[operation])
        left_operand = jnp.concatenate([(weight_col * rotated_real).astype(jnp.bfloat16), (weight_col * rotated_imag).astype(jnp.bfloat16)], 0)
        real_bf = rotated_real.astype(jnp.bfloat16)
        imag_bf = rotated_imag.astype(jnp.bfloat16)
        left_operand, real_bf, imag_bf = lax.optimization_barrier((left_operand, real_bf, imag_bf))
        left_operand = left_operand.astype(jnp.float32)
        real_f = real_bf.astype(jnp.float32)
        imag_f = imag_bf.astype(jnp.float32)
        right_operand = jnp.concatenate([jnp.concatenate([real_f, -imag_f], 1), jnp.concatenate([imag_f, real_f], 1)], 0)
        accumulated = accumulated + jnp.dot(left_operand.T, right_operand, preferred_element_type=jnp.float32, precision=lax.Precision.HIGHEST)
    norm_scale = -1.0 / math.sqrt(NS * PAIRS)
    return jnp.stack([accumulated[:, :NG], accumulated[:, NG:]]) * norm_scale
```

```python
import functools
import math

import jax
import jax.numpy as jnp
from jax import lax
from jax.experimental import pallas as pl
from jax.experimental.pallas import tpu as pltpu
from jax.sharding import PartitionSpec as P

BLOCK = 128
NS = 8
PAIRS = 256
SHARE = 32
WIDE = 768
GROUP = 1536
GROUP_BLOCKS = 12
COL_BLOCKS = 6
SLACK = 2
NORM = -1.0 / math.sqrt(NS * PAIRS)
HALF_ROOT = math.sqrt(0.5)
MESH = pl.DeviceIdType.MESH


def gather_kernel(
    d_ref, w_ref, row_ref, col_ref, wt_ref,
    w_own, c_recv, r_recv, w_recv, w_send, own_send, one_send, two_send, three_send, x_send, z_send, local,
):
    row = lax.axis_index("row")
    col = lax.axis_index("col")
    y, k = row // 2, row % 2
    x, z = col // 4, col % 4
    zp = z % 2
    xn, xb = (x + 1) % 4, (x + 3) % 4
    yn, yb, y2 = (y + 1) % 4, (y + 3) % 4, (y + 2) % 4
    zn, zb = (z + 1) % 4, (z + 3) % 4
    zo = z + 1 - 2 * zp

    def dev(xx, yy, zz, kk):
        return (2 * yy + kk, 4 * xx + zz)

    to_sib = dev(x, y, z, 1 - k)
    to_zo = dev(x, y, zo, k)
    to_yn, to_yb = dev(x, yn, z, k), dev(x, yb, z, k)
    to_xn, to_xb = dev(xn, y, z, k), dev(xb, y, z, k)
    to_zn, to_zb = dev(x, y, zn, k), dev(x, y, zb, k)

    on_line = (z // 2) == k
    dist = (x + 4 - y) % 4
    is_root = jnp.logical_and(on_line, dist == 0)
    is_relay = jnp.logical_and(on_line, dist != 0)
    is_far = jnp.logical_not(on_line)

    def rows_of(yy, kk):
        return pl.ds(pl.multiple_of((2 * yy + kk) * SHARE, SHARE), SHARE)

    def cols_of(zz):
        return pl.ds(pl.multiple_of(zz * WIDE, WIDE), WIDE)

    here = col_ref.at[:, rows_of(y, k), cols_of(zp)]
    get_w = pltpu.make_async_copy(w_ref, w_own, local.at[1])
    get_w.start()
    keep = pltpu.make_async_copy(d_ref, here, local.at[0])
    keep.start()

    barrier = pltpu.get_barrier_semaphore()
    for step in range(1, 8):
        pl.semaphore_signal(barrier, inc=1, device_id=((row + step) % 8, col), device_id_type=MESH)
    for target in (to_xn, to_xb, to_zn, to_zb):
        pl.semaphore_signal(barrier, inc=1, device_id=target, device_id_type=MESH)
    keep.wait()
    pl.semaphore_wait(barrier, 11)

    def copy(src, dst, send, recv, target):
        return pltpu.make_async_remote_copy(
            src_ref=src, dst_ref=dst, send_sem=send, recv_sem=recv, device_id=target, device_id_type=MESH
        )

    def c_copy(yy, kk, zz, send, target, part=None):
        if part is None:
            there = col_ref.at[:, rows_of(yy, kk), cols_of(zz)]
        else:
            there = col_ref.at[part, rows_of(yy, kk), cols_of(zz)]
        recv = c_recv.at[(2 * yy + kk) * 2 + zz, 0 if part is None else part]
        return copy(there, there, send, recv, target)

    def r_copy(yy, zz, send, target, part, src_ref):
        both = pl.ds(pl.multiple_of(yy * 2 * SHARE, 2 * SHARE), 2 * SHARE)
        src = src_ref.at[part, both, cols_of(zz)]
        there = row_ref.at[part, both, cols_of(zz)]
        return copy(src, there, send, r_recv.at[2 * yy + zz, part], target)

    started = []

    def go(desc):
        desc.start()
        started.append(desc)

    go(c_copy(y, k, zp, own_send.at[0], to_zo))
    go(c_copy(y, k, zp, own_send.at[1], to_yn))
    go(c_copy(y, k, zp, own_send.at[2], to_yb))
    go(c_copy(y, k, zp, own_send.at[3], to_sib))

    def chunk(m, first):
        turn = m // 2
        dy = turn + (turn // 2) * (5 - 2 * turn)
        flip = m % 2
        return (y + dy) % 4, first + flip - 2 * first * flip

    def line_copies(m, src_ref):
        yy, zz = chunk(m, zp)
        return (
            lambda: r_copy(yy, zz, x_send.at[m, 0], to_xn, 0, src_ref),
            lambda: r_copy(yy, zz, x_send.at[m, 1], to_xb, 1, src_ref),
            lambda: r_copy(yy, zz, z_send.at[m], to_zn, 0, src_ref),
            lambda: r_copy(yy, zz, z_send.at[m], to_zb, 1, src_ref),
        )

    def root_send(m):
        fwd, bwd, up, down = line_copies(m, col_ref)
        fwd().start()
        bwd().start()

        @pl.when(zp == 1)
        def _():
            up().start()

        @pl.when(zp == 0)
        def _():
            down().start()

    def relay_first(m):
        fwd, _bwd, up, _down = line_copies(m, row_ref)
        fwd().wait_recv()

        @pl.when(dist != 3)
        def _():
            fwd().start()

        @pl.when(zp == 1)
        def _():
            up().start()

    def relay_second(m):
        _fwd, bwd, _up, down = line_copies(m, row_ref)
        bwd().wait_recv()

        @pl.when(dist != 1)
        def _():
            bwd().start()

        @pl.when(zp == 0)
        def _():
            down().start()

    def relay_step(t, carry):
        ahead = t - SLACK * (dist - 1)
        behind = t - SLACK * (3 - dist)

        @pl.when(jnp.logical_and(ahead >= 0, ahead < 8))
        def _():
            relay_first(ahead)

        @pl.when(jnp.logical_and(behind >= 0, behind < 8))
        def _():
            relay_second(behind)

        return carry

    def far_copies(m):
        yy, zz = chunk(m, 1 - zp)
        return (
            lambda: r_copy(yy, zz, z_send.at[m], to_zn, 0, row_ref),
            lambda: r_copy(yy, zz, z_send.at[m], to_zb, 1, row_ref),
        )

    def far_step(m, carry):
        up, down = far_copies(m)

        @pl.when(zp == 0)
        def _():
            up().wait_recv()
            up().start()

        @pl.when(zp == 1)
        def _():
            down().wait_recv()
            down().start()

        return carry

    def line_phase(roots, relays, fars):
        @pl.when(is_root)
        def _():
            for m in roots:
                yy, zz = chunk(m, zp)
                c_copy(yy, 1 - k, zz, own_send.at[0], to_sib).wait_recv()
                root_send(m)

        @pl.when(is_relay)
        def _():
            lax.fori_loop(relays[0], relays[1], relay_step, 0)

        @pl.when(is_far)
        def _():
            lax.fori_loop(fars[0], fars[1], far_step, 0)

    c_copy(y, k, 1 - zp, one_send.at[0], to_zo).wait_recv()
    go(c_copy(y, k, 1 - zp, one_send.at[0], to_yn))
    go(c_copy(y, k, 1 - zp, one_send.at[1], to_yb))
    go(c_copy(y, k, 1 - zp, one_send.at[2], to_sib))

    line_phase((0, 1), (0, 0), (0, 0))

    for flip in range(2):
        zz = zp + flip - 2 * zp * flip
        c_copy(yb, k, zz, own_send.at[0], to_yb).wait_recv()
        go(c_copy(yb, k, zz, two_send.at[flip, 0], to_yn, part=0))
        go(c_copy(yb, k, zz, two_send.at[flip, 1], to_sib))
        c_copy(yn, k, zz, own_send.at[0], to_yn).wait_recv()
        go(c_copy(yn, k, zz, two_send.at[flip, 2], to_yb, part=1))
        go(c_copy(yn, k, zz, two_send.at[flip, 3], to_sib))

    get_w.wait()
    lanes = lax.broadcasted_iota(jnp.int32, (SHARE, SHARE), 1)
    subs = lax.broadcasted_iota(jnp.int32, (SHARE, SHARE), 0)
    spread = jnp.where(lanes == subs, jnp.broadcast_to(w_own[...].astype(jnp.float32), (SHARE, SHARE)), 0.0)
    w_col = jnp.sum(spread, axis=1, keepdims=True)
    my_w = wt_ref.at[pl.ds(pl.multiple_of(row * SHARE, SHARE), SHARE), :]
    my_w[...] = jnp.broadcast_to(w_col, (SHARE, BLOCK)).astype(jnp.bfloat16)
    for step in range(1, 8):
        target = ((row + step) % 8, col)
        go(copy(my_w, my_w, w_send.at[step - 1], w_recv.at[row], target))

    line_phase((2, 3, 4, 5), (0, 4), (0, 2))

    for flip in range(2):
        zz = zp + flip - 2 * zp * flip
        c_copy(y2, k, zz, own_send.at[0], to_yb, part=0).wait_recv()
        c_copy(y2, k, zz, own_send.at[0], to_yn, part=1).wait_recv()
        go(c_copy(y2, k, zz, three_send.at[flip], to_sib))

    line_phase((6, 7), (4, 8 + 2 * SLACK), (2, 8))

    @pl.when(jnp.logical_not(is_root))
    def _():
        for yy in range(4):
            for zz in range(2):
                c_copy(yy, 1 - k, zz, own_send.at[0], to_sib).wait_recv()

    @pl.when(is_root)
    def _():
        row_ref[...] = col_ref[...]

    for step in range(1, 8):
        origin = (row + step) % 8
        theirs = wt_ref.at[pl.ds(pl.multiple_of(origin * SHARE, SHARE), SHARE), :]
        copy(theirs, theirs, w_send.at[0], w_recv.at[origin], to_sib).wait_recv()

    @pl.when(is_far)
    def _():
        def rest(m, carry):
            up, down = far_copies(m)

            @pl.when(zp == 0)
            def _():
                down().wait_recv()

            @pl.when(zp == 1)
            def _():
                up().wait_recv()

            return carry

        lax.fori_loop(0, 8, rest, 0)

    for desc in started:
        desc.wait_send()

    def drain(m, carry):
        @pl.when(on_line)
        def _():
            fwd, bwd, up, _down = line_copies(m, row_ref)

            @pl.when(dist != 3)
            def _():
                fwd().wait_send()

            @pl.when(dist != 1)
            def _():
                bwd().wait_send()

            up().wait_send()

        @pl.when(is_far)
        def _():
            up, _down = far_copies(m)
            up().wait_send()

        return carry

    lax.fori_loop(0, 8, drain, 0)


def gather(densities, weights):
    vmem = pl.BlockSpec(memory_space=pltpu.VMEM)
    hbm = pl.BlockSpec(memory_space=pltpu.HBM)
    dma = pltpu.SemaphoreType.DMA
    return pl.pallas_call(
        gather_kernel,
        out_shape=[
            jax.ShapeDtypeStruct((2, PAIRS, GROUP), jnp.bfloat16),
            jax.ShapeDtypeStruct((2, PAIRS, GROUP), jnp.bfloat16),
            jax.ShapeDtypeStruct((PAIRS, BLOCK), jnp.bfloat16),
        ],
        in_specs=[hbm, hbm],
        out_specs=[vmem, vmem, vmem],
        scratch_shapes=[
            pltpu.VMEM((1, SHARE), jnp.bfloat16),
            dma((16, 2)), dma((8, 2)), dma((8,)), dma((7,)), dma((4,)), dma((3,)),
            dma((2, 4)), dma((2,)), dma((8, 2)), dma((8,)), dma((2,)),
        ],
        compiler_params=pltpu.CompilerParams(
            collective_id=0, has_side_effects=True, vmem_limit_bytes=16 * 2**20
        ),
    )(densities, weights)


def turn_parts(phase):
    odd = jnp.where(phase % 2 == 1, HALF_ROOT, 1.0)
    cos_sign = jnp.where(jnp.logical_or(phase < 2, phase == 7), 1.0, jnp.where(jnp.logical_and(phase > 2, phase < 6), -1.0, 0.0))
    sin_sign = jnp.where(jnp.logical_and(phase > 0, phase < 4), 1.0, jnp.where(phase > 4, -1.0, 0.0))
    return cos_sign * odd, sin_sign * odd


def symmetrize_kernel(
    perm_ref, phase_ref, row_ref, col_ref, wt_ref, out_ref,
    chi, left, right, row_cos, row_sin, col_cos, col_sin,
):
    row = lax.axis_index("row")
    col = lax.axis_index("col")
    b = pl.program_id(0)

    @pl.when(b == 0)
    def _():
        weight = wt_ref[...].astype(jnp.float32) * NORM

        def prepare(t, c):
            tile = pl.ds(pl.multiple_of(t * BLOCK, BLOCK), BLOCK)
            shifted = pl.ds(pl.multiple_of(t * BLOCK + GROUP, BLOCK), BLOCK)
            for part in range(2):
                scaled = row_ref[part, :, tile].astype(jnp.float32) * weight
                left[tile, part * PAIRS:(part + 1) * PAIRS] = scaled.T.astype(jnp.bfloat16)
            right[0:PAIRS, tile] = col_ref[0, :, tile]
            right[PAIRS:2 * PAIRS, tile] = col_ref[1, :, tile]
            right[0:PAIRS, shifted] = -col_ref[1, :, tile]
            right[PAIRS:2 * PAIRS, shifted] = col_ref[0, :, tile]
            return c

        lax.fori_loop(0, GROUP_BLOCKS, prepare, 0)

        def multiply(step, c):
            up, across = step // 3, step % 3
            rows = pl.ds(pl.multiple_of(up * 512, 512), 512)
            cols = pl.ds(pl.multiple_of(across * 1024, 1024), 1024)
            tile = jnp.dot(left[rows, :], right[:, cols], preferred_element_type=jnp.float32)
            for i in range(4):
                for j in range(8):
                    chi[up * 4 + i, across * 8 + j] = tile[i * BLOCK:(i + 1) * BLOCK, j * BLOCK:(j + 1) * BLOCK]
            return c

        lax.fori_loop(0, 9, multiply, 0)

        phases = phase_ref[:, pl.ds(pl.multiple_of(col * WIDE, BLOCK), WIDE)]
        cosine, sine = turn_parts(phases)
        for s in range(NS):
            for c in range(COL_BLOCKS):
                lane = slice(c * BLOCK, (c + 1) * BLOCK)
                col_cos[s, c] = jnp.broadcast_to(cosine[s:s + 1, lane], (8, BLOCK))
                col_sin[s, c] = jnp.broadcast_to(sine[s:s + 1, lane], (8, BLOCK))

    phases = phase_ref[:, pl.ds(pl.multiple_of(row * GROUP + b * BLOCK, BLOCK), BLOCK)]
    cosine, sine = turn_parts(phases)
    cosine, sine = cosine.T, sine.T
    for s in range(NS):
        row_cos[s] = jnp.broadcast_to(cosine[:, s:s + 1], (BLOCK, BLOCK))
        row_sin[s] = jnp.broadcast_to(sine[:, s:s + 1], (BLOCK, BLOCK))

    row_from = [perm_ref[s, row * GROUP_BLOCKS + b] - row * GROUP_BLOCKS for s in range(NS)]
    col_group = (col // 2) * GROUP_BLOCKS

    def column(c, carry):
        col_from = [perm_ref[s, col * COL_BLOCKS + c] - col_group for s in range(NS)]
        here = pl.ds(pl.multiple_of(c * BLOCK, BLOCK), BLOCK)

        for t in range(BLOCK // 8):
            rows = slice(t * 8, (t + 1) * 8)
            real = imag = None
            for s in range(NS):
                xr = chi[row_from[s], col_from[s], rows]
                xi = chi[row_from[s], col_from[s] + GROUP_BLOCKS, rows]
                cg, sg = row_cos[s, rows], row_sin[s, rows]
                ch, sh = col_cos[s, c], col_sin[s, c]
                turn_c = cg * ch + sg * sh
                turn_s = sg * ch - cg * sh
                add_r = turn_c * xr - turn_s * xi
                add_i = turn_c * xi + turn_s * xr
                real = add_r if s == 0 else real + add_r
                imag = add_i if s == 0 else imag + add_i
            out_ref[0, rows, here] = real
            out_ref[1, rows, here] = imag
        return carry

    lax.fori_loop(0, COL_BLOCKS, column, 0)


def symmetrize(block_perm, phase_index, row_all, col_all, weights):
    vmem = pl.BlockSpec(memory_space=pltpu.VMEM)
    bf16, f32 = jnp.bfloat16, jnp.float32
    return pl.pallas_call(
        symmetrize_kernel,
        grid=(GROUP_BLOCKS,),
        out_shape=jax.ShapeDtypeStruct((2, GROUP, WIDE), f32),
        in_specs=[pl.BlockSpec(memory_space=pltpu.SMEM), vmem, vmem, vmem, vmem],
        out_specs=pl.BlockSpec((2, BLOCK, WIDE), lambda b: (0, b, 0)),
        scratch_shapes=[
            pltpu.VMEM((GROUP_BLOCKS, 2 * GROUP_BLOCKS, BLOCK, BLOCK), f32),
            pltpu.VMEM((GROUP, 2 * PAIRS), bf16),
            pltpu.VMEM((2 * PAIRS, 2 * GROUP), bf16),
            pltpu.VMEM((NS, BLOCK, BLOCK), f32),
            pltpu.VMEM((NS, BLOCK, BLOCK), f32),
            pltpu.VMEM((NS, COL_BLOCKS, 8, BLOCK), f32),
            pltpu.VMEM((NS, COL_BLOCKS, 8, BLOCK), f32),
        ],
        compiler_params=pltpu.CompilerParams(vmem_limit_bytes=48 * 2**20),
    )(block_perm, phase_index, row_all, col_all, weights)


def shards(densities, pair_weight, block_perm, phase_index):
    row_all, col_all, weights = gather(densities, pair_weight.reshape(1, SHARE))
    return symmetrize(block_perm, phase_index, row_all, col_all, weights)


def solution(mesh):
    return jax.shard_map(
        shards,
        mesh=mesh,
        in_specs=(P(None, "row", "col"), P("row"), P(), P()),
        out_specs=P(None, "row", "col"),
        check_vma=False,
    )
```

```python
import functools
import math

import jax
import jax.numpy as jnp
from jax import lax
from jax.experimental import pallas as pl
from jax.experimental.pallas import tpu as pltpu
from jax.sharding import PartitionSpec as P

BLOCK = 128
NS = 8
PAIRS = 256
SHARE = 32
WIDE = 768
GROUP = 1536
GROUP_BLOCKS = 12
COL_BLOCKS = 6
FAR_LAG = 2
GATHER_VMEM = 16 * 2**20
NORM = -1.0 / math.sqrt(NS * PAIRS)
HALF_ROOT = math.sqrt(0.5)
MESH = pl.DeviceIdType.MESH


def gather_kernel(
    d_ref, w_ref, hop_ref, col_ref, wt_ref,
    w_own, c_recv, line_recv, far_recv, sib_recv, mate_recv, w_recv, bulk, sib_send, cross_send,
    mate_send, w_send, local,
):
    row = lax.axis_index("row")
    col = lax.axis_index("col")
    y, k = row // 2, row % 2
    x, z = col // 4, col % 4
    zp, q = z % 2, z // 2
    zo = z + 1 - 2 * zp
    zc = (z + 3 + 2 * zp) % 4

    def dev(xx, yy, zz, kk):
        return (2 * yy + kk, 4 * xx + zz)

    on_line = q == k
    is_root = x == y
    to_sib = dev(x, y, z, 1 - k)
    to_zo = dev(x, y, zo, k)
    to_cross = dev(x, y, zc, q)

    def rows_of(yy, kk):
        return pl.ds(pl.multiple_of((2 * yy + kk) * SHARE, SHARE), SHARE)

    def pair_of(yy):
        return pl.ds(pl.multiple_of(yy * 2 * SHARE, 2 * SHARE), 2 * SHARE)

    def cols_of(zz):
        return pl.ds(pl.multiple_of(zz * WIDE, WIDE), WIDE)

    get_w = pltpu.make_async_copy(w_ref, w_own, local.at[1])
    get_w.start()
    keep = pltpu.make_async_copy(d_ref, col_ref.at[:, rows_of(y, k), cols_of(zp)], local.at[0])
    keep.start()

    barrier = pltpu.get_barrier_semaphore()

    def greet(target):
        pl.semaphore_signal(barrier, inc=1, device_id=target, device_id_type=MESH)

    for step in range(1, 8):
        greet(((row + step) % 8, col))
    greet(to_zo)

    @pl.when(jnp.logical_not(is_root))
    def _():
        for yy in range(4):
            greet(dev(y, yy, z, k))

    @pl.when(jnp.logical_not(on_line))
    def _():
        greet(dev(x, y, zc, 0))
        greet(dev(x, y, zc, 1))

    pl.semaphore_wait(barrier, 12)

    def copy(src, dst, send, recv, target):
        return pltpu.make_async_remote_copy(
            src_ref=src, dst_ref=dst, send_sem=send, recv_sem=recv, device_id=target, device_id_type=MESH
        )

    def c_at(yy, zz):
        return col_ref.at[:, rows_of(yy, k), cols_of(zz)]

    def r_at(which, yy, zz):
        return hop_ref.at[which, :, rows_of(yy, k), cols_of(zz)]

    def c_copy(yy, zz, target, src=None):
        there = c_at(yy, zz)
        return copy(there if src is None else src, there, bulk.at[0], c_recv.at[2 * yy + zz], target)

    def spread_block(zz, src):
        for step in range(1, 4):
            target = dev((x + step) % 4, x, z, k)
            copy(src, r_at(q, y, zz), bulk.at[0], line_recv.at[2 * y + zz], target).start()
        for step in range(4):
            yy = (x + step) % 4

            @pl.when(yy != y)
            def _():
                c_copy(y, zz, dev(x, yy, z, k), src).start()

    c_copy(y, zp, to_zo, d_ref).start()
    spread_block(zp, d_ref)
    keep.wait()
    c_copy(y, 1 - zp, to_zo).wait_recv()
    spread_block(1 - zp, c_at(y, 1 - zp))

    def sib_c(yy, kk):
        there = col_ref.at[:, rows_of(yy, kk), :]
        return copy(there, there, sib_send.at[0], sib_recv.at[yy], to_sib)

    sib_c(y, k).start()

    get_w.wait()
    lanes = lax.broadcasted_iota(jnp.int32, (SHARE, SHARE), 1)
    subs = lax.broadcasted_iota(jnp.int32, (SHARE, SHARE), 0)
    spread = jnp.where(lanes == subs, jnp.broadcast_to(w_own[...].astype(jnp.float32), (SHARE, SHARE)), 0.0)
    w_col = jnp.sum(spread, axis=1, keepdims=True)

    def w_at(origin):
        return wt_ref.at[pl.ds(pl.multiple_of(origin * SHARE, SHARE), SHARE), :]

    w_at(row)[...] = jnp.broadcast_to(w_col, (SHARE, BLOCK)).astype(jnp.bfloat16)
    for step in range(1, 8):
        target = ((row + step) % 8, col)
        copy(w_at(row), w_at(row), w_send.at[0], w_recv.at[row], target).start()

    def cross(yy, zz, part, from_col):
        there = hop_ref.at[q, part, rows_of(yy, k), cols_of(zz)]
        src = col_ref.at[part, rows_of(yy, k), cols_of(zz)] if from_col else there
        return copy(src, there, cross_send.at[0], far_recv.at[2 * yy + zz], to_cross)

    def cross_start(yy, zz, from_col):
        @pl.when(zp == 1)
        def _():
            cross(yy, zz, 0, from_col).start()

        @pl.when(zp == 0)
        def _():
            cross(yy, zz, 1, from_col).start()

    def sib_r(yy, zz):
        return copy(r_at(q, yy, zz), r_at(q, yy, zz), sib_send.at[1], sib_recv.at[4], to_sib)

    def line(n):
        yy = (y + n % 4) % 4
        zz = zp if n < 4 else 1 - zp

        @pl.when(is_root)
        def _():
            if n % 4 != 0:
                c_copy(yy, zz, to_zo).wait_recv()
            cross_start(yy, zz, True)
            if n > 4:
                sib_c(yy, k).start()

        @pl.when(jnp.logical_not(is_root))
        def _():
            copy(r_at(q, yy, zz), r_at(q, yy, zz), bulk.at[0], line_recv.at[2 * yy + zz], to_zo).wait_recv()
            cross_start(yy, zz, False)

            @pl.when(jnp.logical_not(on_line))
            def _():
                sib_r(yy, zz).start()

    def mate(yy, zz, part):
        there = hop_ref.at[k, part, pair_of(yy), cols_of(zz)]
        return copy(there, there, mate_send.at[0], mate_recv.at[0], to_zo)

    def far(n):
        yy = (y + n % 4) % 4
        zz = 1 - zp if n < 4 else zp

        def arrive(part):
            there = hop_ref.at[k, part, pair_of(yy), cols_of(zz)]
            copy(there, there, mate_send.at[0], far_recv.at[2 * yy + zz], to_zo).wait_recv()
            mate(yy, zz, part).start()

        @pl.when(jnp.logical_and(jnp.logical_not(on_line), zp == 0))
        def _():
            arrive(0)

        @pl.when(jnp.logical_and(jnp.logical_not(on_line), zp == 1))
        def _():
            arrive(1)

    for step in range(8 + FAR_LAG):
        if step < 8:
            line(step)
        if step >= FAR_LAG:
            far(step - FAR_LAG)

    @pl.when(jnp.logical_not(is_root))
    def _():
        for step in range(1, 4):
            yy = (y + step) % 4
            c_copy(yy, 0, to_zo).wait_recv()
            c_copy(yy, 1, to_zo).wait_recv()
            sib_c(yy, k).start()

    for yy in range(4):
        sib_c(yy, 1 - k).wait_recv()

    half = hop_ref.at[k, :, 0:PAIRS // 2, :]
    whole = hop_ref.at[k, 0]

    @pl.when(jnp.logical_not(on_line))
    def _():
        copy(whole, whole, mate_send.at[0], mate_recv.at[0], to_zo).wait_recv()

    @pl.when(jnp.logical_and(on_line, jnp.logical_not(is_root)))
    def _():
        copy(half, half, sib_send.at[1], sib_recv.at[4], to_sib).wait_recv()

    @pl.when(jnp.logical_and(on_line, is_root))
    def _():
        hop_ref[k] = col_ref[...]

    for step in range(1, 8):
        origin = (row + step) % 8
        copy(w_at(origin), w_at(origin), w_send.at[0], w_recv.at[origin], to_sib).wait_recv()

    sent = col_ref.at[:, 0:208, :]
    copy(sent, sent, bulk.at[0], c_recv.at[0], to_zo).wait_send()
    copy(half, half, sib_send.at[0], sib_recv.at[0], to_sib).wait_send()
    part_half = hop_ref.at[k, 0, 0:PAIRS // 2, :]
    copy(part_half, part_half, cross_send.at[0], far_recv.at[0], to_zo).wait_send()
    w_sent = wt_ref.at[0:7 * SHARE, :]
    copy(w_sent, w_sent, w_send.at[0], w_recv.at[0], to_sib).wait_send()

    @pl.when(jnp.logical_not(on_line))
    def _():
        copy(whole, whole, mate_send.at[0], mate_recv.at[0], to_zo).wait_send()

        @pl.when(jnp.logical_not(is_root))
        def _():
            copy(half, half, sib_send.at[1], sib_recv.at[4], to_sib).wait_send()


def gather(densities, weights):
    vmem = pl.BlockSpec(memory_space=pltpu.VMEM)
    hbm = pl.BlockSpec(memory_space=pltpu.HBM)
    dma = pltpu.SemaphoreType.DMA
    return pl.pallas_call(
        gather_kernel,
        out_shape=[
            jax.ShapeDtypeStruct((2, 2, PAIRS, GROUP), jnp.bfloat16),
            jax.ShapeDtypeStruct((2, PAIRS, GROUP), jnp.bfloat16),
            jax.ShapeDtypeStruct((PAIRS, BLOCK), jnp.bfloat16),
        ],
        in_specs=[hbm, hbm],
        out_specs=[vmem, vmem, vmem],
        scratch_shapes=[
            pltpu.VMEM((1, SHARE), jnp.bfloat16),
            dma((8,)), dma((8,)), dma((8,)), dma((5,)), dma((1,)), dma((8,)), dma((1,)), dma((2,)), dma((1,)),
            dma((1,)), dma((1,)), dma((2,)),
        ],
        compiler_params=pltpu.CompilerParams(
            collective_id=0, has_side_effects=True, vmem_limit_bytes=GATHER_VMEM
        ),
    )(densities, weights)


def turn_parts(phase):
    odd = jnp.where(phase % 2 == 1, HALF_ROOT, 1.0)
    cos_sign = jnp.where(jnp.logical_or(phase < 2, phase == 7), 1.0, jnp.where(jnp.logical_and(phase > 2, phase < 6), -1.0, 0.0))
    sin_sign = jnp.where(jnp.logical_and(phase > 0, phase < 4), 1.0, jnp.where(phase > 4, -1.0, 0.0))
    return cos_sign * odd, sin_sign * odd


def symmetrize_kernel(
    perm_ref, phase_ref, hop_ref, col_ref, wt_ref, out_ref,
    chi, left, right, spread, turns, col_cos, col_sin,
):
    row = lax.axis_index("row")
    col = lax.axis_index("col")
    b = pl.program_id(0)

    @pl.when(b == 0)
    def _():
        entry = lax.broadcasted_iota(jnp.int32, (4 * NS, 2 * NS * BLOCK), 0) % (2 * NS)
        block = lax.broadcasted_iota(jnp.int32, (4 * NS, 2 * NS * BLOCK), 1) // BLOCK
        spread[...] = jnp.where(entry == block, 1.0, 0.0).astype(jnp.bfloat16)

        phases = phase_ref[:, pl.ds(pl.multiple_of(col * WIDE, BLOCK), WIDE)]
        cosine, sine = turn_parts(phases)
        for s in range(NS):
            for c in range(COL_BLOCKS):
                lane = slice(c * BLOCK, (c + 1) * BLOCK)
                col_cos[s, c] = jnp.broadcast_to(cosine[s:s + 1, lane], (8, BLOCK))
                col_sin[s, c] = jnp.broadcast_to(sine[s:s + 1, lane], (8, BLOCK))

        weight = wt_ref[...].astype(jnp.float32) * NORM

        def prepare_left(t, c):
            tile = pl.ds(pl.multiple_of(t * BLOCK, BLOCK), BLOCK)
            for part in range(2):
                scaled = hop_ref[row % 2, part, :, tile].astype(jnp.float32) * weight
                left[tile, part * PAIRS:(part + 1) * PAIRS] = scaled.T.astype(jnp.bfloat16)
            return c

        lax.fori_loop(0, GROUP_BLOCKS, prepare_left, 0, unroll=2)
        right[0:PAIRS, 0:GROUP] = col_ref[0]
        right[PAIRS:2 * PAIRS, 0:GROUP] = col_ref[1]
        right[0:PAIRS, GROUP:2 * GROUP] = -col_ref[1]
        right[PAIRS:2 * PAIRS, GROUP:2 * GROUP] = col_ref[0]

        def multiply(up, c):
            rows = pl.ds(pl.multiple_of(up * 512, 512), 512)
            tile = jnp.dot(left[rows, :], right[...], preferred_element_type=jnp.float32)
            for i in range(4):
                for j in range(2 * GROUP_BLOCKS):
                    chi[up * 4 + i, j] = tile[i * BLOCK:(i + 1) * BLOCK, j * BLOCK:(j + 1) * BLOCK]
            return c

        lax.fori_loop(0, 3, multiply, 0)

    phases = phase_ref[:, pl.ds(pl.multiple_of(row * GROUP + b * BLOCK, BLOCK), BLOCK)]
    both = jnp.concatenate(turn_parts(phases), axis=0)
    coarse = both.astype(jnp.bfloat16).astype(jnp.float32)
    pieces = jnp.concatenate([coarse, both - coarse], axis=0).T.astype(jnp.bfloat16)
    turns[...] = jnp.dot(pieces, spread[...], preferred_element_type=jnp.float32)

    row_from = [perm_ref[s, row * GROUP_BLOCKS + b] - row * GROUP_BLOCKS for s in range(NS)]
    col_group = (col // 2) * GROUP_BLOCKS

    def column(c, carry):
        col_from = [perm_ref[s, col * COL_BLOCKS + c] - col_group for s in range(NS)]
        here = pl.ds(pl.multiple_of(c * BLOCK, BLOCK), BLOCK)

        for t in range(BLOCK // 8):
            rows = slice(t * 8, (t + 1) * 8)
            real = imag = None
            for s in range(NS):
                xr = chi[row_from[s], col_from[s], rows]
                xi = chi[row_from[s], col_from[s] + GROUP_BLOCKS, rows]
                cg = turns[rows, s * BLOCK:(s + 1) * BLOCK]
                sg = turns[rows, (NS + s) * BLOCK:(NS + s + 1) * BLOCK]
                ch, sh = col_cos[s, c], col_sin[s, c]
                turn_c = cg * ch + sg * sh
                turn_s = sg * ch - cg * sh
                add_r = turn_c * xr - turn_s * xi
                add_i = turn_c * xi + turn_s * xr
                real = add_r if s == 0 else real + add_r
                imag = add_i if s == 0 else imag + add_i
            out_ref[0, rows, here] = real
            out_ref[1, rows, here] = imag
        return carry

    lax.fori_loop(0, COL_BLOCKS, column, 0, unroll=2)


def symmetrize(block_perm, phase_index, row_all, col_all, weights):
    vmem = pl.BlockSpec(memory_space=pltpu.VMEM)
    bf16, f32 = jnp.bfloat16, jnp.float32
    return pl.pallas_call(
        symmetrize_kernel,
        grid=(GROUP_BLOCKS,),
        out_shape=jax.ShapeDtypeStruct((2, GROUP, WIDE), f32),
        in_specs=[pl.BlockSpec(memory_space=pltpu.SMEM), vmem, vmem, vmem, vmem],
        out_specs=pl.BlockSpec((2, BLOCK, WIDE), lambda b: (0, b, 0)),
        scratch_shapes=[
            pltpu.VMEM((GROUP_BLOCKS, 2 * GROUP_BLOCKS, BLOCK, BLOCK), f32),
            pltpu.VMEM((GROUP, 2 * PAIRS), bf16),
            pltpu.VMEM((2 * PAIRS, 2 * GROUP), bf16),
            pltpu.VMEM((4 * NS, 2 * NS * BLOCK), bf16),
            pltpu.VMEM((BLOCK, 2 * NS * BLOCK), f32),
            pltpu.VMEM((NS, COL_BLOCKS, 8, BLOCK), f32),
            pltpu.VMEM((NS, COL_BLOCKS, 8, BLOCK), f32),
        ],
        compiler_params=pltpu.CompilerParams(vmem_limit_bytes=48 * 2**20),
    )(block_perm, phase_index, row_all, col_all, weights)


def shards(densities, pair_weight, block_perm, phase_index):
    row_all, col_all, weights = gather(densities, pair_weight.reshape(1, SHARE))
    return symmetrize(block_perm, phase_index, row_all, col_all, weights)


def solution(mesh):
    return jax.shard_map(
        shards,
        mesh=mesh,
        in_specs=(P(None, "row", "col"), P("row"), P(), P()),
        out_specs=P(None, "row", "col"),
        check_vma=False,
    )
```

```python
import functools
import math

import jax
import jax.numpy as jnp
from jax import lax
from jax.experimental import pallas as pl
from jax.experimental.pallas import tpu as pltpu
from jax.sharding import PartitionSpec as P

BLOCK = 128
NS = 8
PAIRS = 256
SHARE = 32
WIDE = 768
GROUP = 1536
GROUP_BLOCKS = 12
COL_BLOCKS = 6
FAR_LAG = 2
GATHER_VMEM = 16 * 2**20
NORM = -1.0 / math.sqrt(NS * PAIRS)
HALF_ROOT = math.sqrt(0.5)
MESH = pl.DeviceIdType.MESH


def turn_parts(phase):
    odd = jnp.where(phase % 2 == 1, HALF_ROOT, 1.0)
    cos_sign = jnp.where(jnp.logical_or(phase < 2, phase == 7), 1.0, jnp.where(jnp.logical_and(phase > 2, phase < 6), -1.0, 0.0))
    sin_sign = jnp.where(jnp.logical_and(phase > 0, phase < 4), 1.0, jnp.where(phase > 4, -1.0, 0.0))
    return cos_sign * odd, sin_sign * odd


def gather_kernel(
    d_ref, w_ref, phase_ref, hop_ref, col_ref, wt_ref, row_turns, col_turns,
    w_own, c_recv, line_recv, far_recv, sib_recv, mate_recv, w_recv, bulk, sib_send, cross_send,
    mate_send, w_send, local,
):
    row = lax.axis_index("row")
    col = lax.axis_index("col")
    y, k = row // 2, row % 2
    x, z = col // 4, col % 4
    zp, q = z % 2, z // 2
    zo = z + 1 - 2 * zp
    zc = (z + 3 + 2 * zp) % 4

    def dev(xx, yy, zz, kk):
        return (2 * yy + kk, 4 * xx + zz)

    on_line = q == k
    is_root = x == y
    to_sib = dev(x, y, z, 1 - k)
    to_zo = dev(x, y, zo, k)
    to_cross = dev(x, y, zc, q)

    def rows_of(yy, kk):
        return pl.ds(pl.multiple_of((2 * yy + kk) * SHARE, SHARE), SHARE)

    def pair_of(yy):
        return pl.ds(pl.multiple_of(yy * 2 * SHARE, 2 * SHARE), 2 * SHARE)

    def cols_of(zz):
        return pl.ds(pl.multiple_of(zz * WIDE, WIDE), WIDE)

    get_w = pltpu.make_async_copy(w_ref, w_own, local.at[1])
    get_w.start()
    keep = pltpu.make_async_copy(d_ref, col_ref.at[:, rows_of(y, k), cols_of(zp)], local.at[0])
    keep.start()

    barrier = pltpu.get_barrier_semaphore()

    def greet(target):
        pl.semaphore_signal(barrier, inc=1, device_id=target, device_id_type=MESH)

    for step in range(1, 8):
        greet(((row + step) % 8, col))
    greet(to_zo)

    @pl.when(jnp.logical_not(is_root))
    def _():
        for yy in range(4):
            greet(dev(y, yy, z, k))

    @pl.when(jnp.logical_not(on_line))
    def _():
        greet(dev(x, y, zc, 0))
        greet(dev(x, y, zc, 1))

    pl.semaphore_wait(barrier, 12)

    def copy(src, dst, send, recv, target):
        return pltpu.make_async_remote_copy(
            src_ref=src, dst_ref=dst, send_sem=send, recv_sem=recv, device_id=target, device_id_type=MESH
        )

    def c_at(yy, zz):
        return col_ref.at[:, rows_of(yy, k), cols_of(zz)]

    def r_at(which, yy, zz):
        return hop_ref.at[which, :, rows_of(yy, k), cols_of(zz)]

    def c_copy(yy, zz, target, src=None):
        there = c_at(yy, zz)
        return copy(there if src is None else src, there, bulk.at[0], c_recv.at[2 * yy + zz], target)

    def spread_block(zz, src):
        for step in range(1, 4):
            target = dev((x + step) % 4, x, z, k)
            copy(src, r_at(q, y, zz), bulk.at[0], line_recv.at[2 * y + zz], target).start()
        for step in range(4):
            yy = (x + step) % 4

            @pl.when(yy != y)
            def _():
                c_copy(y, zz, dev(x, yy, z, k), src).start()

    c_copy(y, zp, to_zo, d_ref).start()
    spread_block(zp, d_ref)

    cosine, sine = turn_parts(phase_ref[:, pl.ds(pl.multiple_of(col * WIDE, BLOCK), WIDE)])
    col_turns[0] = cosine
    col_turns[1] = sine

    def row_block(b, carry):
        phases = phase_ref[:, pl.ds(pl.multiple_of(row * GROUP + b * BLOCK, BLOCK), BLOCK)]
        both = jnp.concatenate(turn_parts(phases), axis=0)
        coarse = both.astype(jnp.bfloat16).astype(jnp.float32)
        pieces = jnp.concatenate([coarse, both - coarse], axis=0).T.astype(jnp.bfloat16)
        row_turns[pl.ds(pl.multiple_of(b * BLOCK, BLOCK), BLOCK), :] = pieces
        return carry

    lax.fori_loop(0, GROUP_BLOCKS, row_block, 0)
    keep.wait()
    c_copy(y, 1 - zp, to_zo).wait_recv()
    spread_block(1 - zp, c_at(y, 1 - zp))

    def sib_c(yy, kk):
        there = col_ref.at[:, rows_of(yy, kk), :]
        return copy(there, there, sib_send.at[0], sib_recv.at[yy], to_sib)

    sib_c(y, k).start()

    get_w.wait()
    lanes = lax.broadcasted_iota(jnp.int32, (SHARE, SHARE), 1)
    subs = lax.broadcasted_iota(jnp.int32, (SHARE, SHARE), 0)
    spread = jnp.where(lanes == subs, jnp.broadcast_to(w_own[...].astype(jnp.float32), (SHARE, SHARE)), 0.0)
    w_col = jnp.sum(spread, axis=1, keepdims=True)

    def w_at(origin):
        return wt_ref.at[pl.ds(pl.multiple_of(origin * SHARE, SHARE), SHARE), :]

    w_at(row)[...] = jnp.broadcast_to(w_col, (SHARE, BLOCK)).astype(jnp.bfloat16)
    for step in range(1, 8):
        target = ((row + step) % 8, col)
        copy(w_at(row), w_at(row), w_send.at[0], w_recv.at[row], target).start()

    def cross(yy, zz, part, from_col):
        there = hop_ref.at[q, part, rows_of(yy, k), cols_of(zz)]
        src = col_ref.at[part, rows_of(yy, k), cols_of(zz)] if from_col else there
        return copy(src, there, cross_send.at[0], far_recv.at[2 * yy + zz], to_cross)

    def cross_start(yy, zz, from_col):
        @pl.when(zp == 1)
        def _():
            cross(yy, zz, 0, from_col).start()

        @pl.when(zp == 0)
        def _():
            cross(yy, zz, 1, from_col).start()

    def cross_both(yy, zz):
        return copy(c_at(yy, zz), r_at(q, yy, zz), cross_send.at[0], far_recv.at[2 * yy + zz], to_cross)

    def sib_r(yy, zz):
        return copy(r_at(q, yy, zz), r_at(q, yy, zz), sib_send.at[1], sib_recv.at[4], to_sib)

    def line(n):
        yy = (y + n % 4) % 4
        zz = zp if n < 4 else 1 - zp

        @pl.when(is_root)
        def _():
            if n % 4 != 0:
                c_copy(yy, zz, to_zo).wait_recv()
            if n % 4 == 2:
                cross_both(yy, zz).start()
            else:
                cross_start(yy, zz, True)
            if n > 4:
                sib_c(yy, k).start()

        @pl.when(jnp.logical_not(is_root))
        def _():
            copy(r_at(q, yy, zz), r_at(q, yy, zz), bulk.at[0], line_recv.at[2 * yy + zz], to_zo).wait_recv()
            cross_start(yy, zz, False)

            @pl.when(jnp.logical_not(on_line))
            def _():
                sib_r(yy, zz).start()

    def mate(yy, zz, part):
        there = hop_ref.at[k, part, pair_of(yy), cols_of(zz)]
        return copy(there, there, mate_send.at[0], mate_recv.at[0], to_zo)

    def far(n):
        yy = (y + n % 4) % 4
        zz = 1 - zp if n < 4 else zp

        def arrive(part):
            there = hop_ref.at[k, part, pair_of(yy), cols_of(zz)]
            copy(there, there, mate_send.at[0], far_recv.at[2 * yy + zz], to_zo).wait_recv()
            mate(yy, zz, part).start()

        relayed = jnp.logical_not(on_line)
        if n % 4 == 2:
            @pl.when(jnp.logical_and(relayed, is_root))
            def _():
                there = hop_ref.at[k, :, pair_of(yy), cols_of(zz)]
                copy(there, there, mate_send.at[0], far_recv.at[2 * yy + zz], to_zo).wait_recv()

            relayed = jnp.logical_and(relayed, jnp.logical_not(is_root))

        @pl.when(jnp.logical_and(relayed, zp == 0))
        def _():
            arrive(0)

        @pl.when(jnp.logical_and(relayed, zp == 1))
        def _():
            arrive(1)

    for step in range(8 + FAR_LAG):
        if step < 8:
            line(step)
        if step >= FAR_LAG:
            far(step - FAR_LAG)

    @pl.when(jnp.logical_not(is_root))
    def _():
        for step in range(1, 4):
            yy = (y + step) % 4
            c_copy(yy, 0, to_zo).wait_recv()
            c_copy(yy, 1, to_zo).wait_recv()
            sib_c(yy, k).start()

    for yy in range(4):
        sib_c(yy, 1 - k).wait_recv()

    half = hop_ref.at[k, :, 0:PAIRS // 2, :]
    whole = hop_ref.at[k, 0]
    most = hop_ref.at[k, 0, 0:3 * PAIRS // 4, :]
    far_root = jnp.logical_and(jnp.logical_not(on_line), is_root)
    far_other = jnp.logical_and(jnp.logical_not(on_line), jnp.logical_not(is_root))

    @pl.when(far_root)
    def _():
        copy(most, most, mate_send.at[0], mate_recv.at[0], to_zo).wait_recv()

    @pl.when(far_other)
    def _():
        copy(whole, whole, mate_send.at[0], mate_recv.at[0], to_zo).wait_recv()

    @pl.when(jnp.logical_and(on_line, jnp.logical_not(is_root)))
    def _():
        copy(half, half, sib_send.at[1], sib_recv.at[4], to_sib).wait_recv()

    @pl.when(jnp.logical_and(on_line, is_root))
    def _():
        hop_ref[k] = col_ref[...]

    for step in range(1, 8):
        origin = (row + step) % 8
        copy(w_at(origin), w_at(origin), w_send.at[0], w_recv.at[origin], to_sib).wait_recv()

    sent = col_ref.at[:, 0:208, :]
    copy(sent, sent, bulk.at[0], c_recv.at[0], to_zo).wait_send()
    copy(half, half, sib_send.at[0], sib_recv.at[0], to_sib).wait_send()
    part_half = hop_ref.at[k, 0, 0:PAIRS // 2, :]
    part_more = hop_ref.at[k, 0, 0:5 * PAIRS // 8, :]

    @pl.when(is_root)
    def _():
        copy(part_more, part_more, cross_send.at[0], far_recv.at[0], to_zo).wait_send()

    @pl.when(jnp.logical_not(is_root))
    def _():
        copy(part_half, part_half, cross_send.at[0], far_recv.at[0], to_zo).wait_send()

    w_sent = wt_ref.at[0:7 * SHARE, :]
    copy(w_sent, w_sent, w_send.at[0], w_recv.at[0], to_sib).wait_send()

    @pl.when(far_root)
    def _():
        copy(most, most, mate_send.at[0], mate_recv.at[0], to_zo).wait_send()

    @pl.when(far_other)
    def _():
        copy(whole, whole, mate_send.at[0], mate_recv.at[0], to_zo).wait_send()
        copy(half, half, sib_send.at[1], sib_recv.at[4], to_sib).wait_send()


def gather(densities, weights, phase_index):
    vmem = pl.BlockSpec(memory_space=pltpu.VMEM)
    hbm = pl.BlockSpec(memory_space=pltpu.HBM)
    dma = pltpu.SemaphoreType.DMA
    return pl.pallas_call(
        gather_kernel,
        out_shape=[
            jax.ShapeDtypeStruct((2, 2, PAIRS, GROUP), jnp.bfloat16),
            jax.ShapeDtypeStruct((2, PAIRS, GROUP), jnp.bfloat16),
            jax.ShapeDtypeStruct((PAIRS, BLOCK), jnp.bfloat16),
            jax.ShapeDtypeStruct((GROUP, 4 * NS), jnp.bfloat16),
            jax.ShapeDtypeStruct((2, NS, WIDE), jnp.float32),
        ],
        in_specs=[hbm, hbm, vmem],
        out_specs=[vmem, vmem, vmem, vmem, vmem],
        scratch_shapes=[
            pltpu.VMEM((1, SHARE), jnp.bfloat16),
            dma((8,)), dma((8,)), dma((8,)), dma((5,)), dma((1,)), dma((8,)), dma((1,)), dma((2,)), dma((1,)),
            dma((1,)), dma((1,)), dma((2,)),
        ],
        compiler_params=pltpu.CompilerParams(
            collective_id=0, has_side_effects=True, vmem_limit_bytes=GATHER_VMEM
        ),
    )(densities, weights, phase_index)


def symmetrize_kernel(
    perm_ref, row_turns, col_turns, hop_ref, col_ref, wt_ref, out_ref,
    chi, left, right, spread, turns, col_cos, col_sin,
):
    row = lax.axis_index("row")
    col = lax.axis_index("col")
    b = pl.program_id(0)

    @pl.when(b == 0)
    def _():
        entry = lax.broadcasted_iota(jnp.int32, (4 * NS, 2 * NS * BLOCK), 0) % (2 * NS)
        block = lax.broadcasted_iota(jnp.int32, (4 * NS, 2 * NS * BLOCK), 1) // BLOCK
        spread[...] = jnp.where(entry == block, 1.0, 0.0).astype(jnp.bfloat16)

        cosine, sine = col_turns[0], col_turns[1]
        for s in range(NS):
            for c in range(COL_BLOCKS):
                lane = slice(c * BLOCK, (c + 1) * BLOCK)
                col_cos[s, c] = jnp.broadcast_to(cosine[s:s + 1, lane], (8, BLOCK))
                col_sin[s, c] = jnp.broadcast_to(sine[s:s + 1, lane], (8, BLOCK))

        weight = wt_ref[...].astype(jnp.float32) * NORM

        def prepare_left(t, c):
            tile = pl.ds(pl.multiple_of(t * BLOCK, BLOCK), BLOCK)
            for part in range(2):
                scaled = hop_ref[row % 2, part, :, tile].astype(jnp.float32) * weight
                left[tile, part * PAIRS:(part + 1) * PAIRS] = scaled.T.astype(jnp.bfloat16)
            return c

        lax.fori_loop(0, GROUP_BLOCKS, prepare_left, 0, unroll=2)
        right[0:PAIRS, 0:GROUP] = col_ref[0]
        right[PAIRS:2 * PAIRS, 0:GROUP] = col_ref[1]
        right[0:PAIRS, GROUP:2 * GROUP] = -col_ref[1]
        right[PAIRS:2 * PAIRS, GROUP:2 * GROUP] = col_ref[0]

        def multiply(up, c):
            rows = pl.ds(pl.multiple_of(up * 512, 512), 512)
            tile = jnp.dot(left[rows, :], right[...], preferred_element_type=jnp.float32)
            for i in range(4):
                for j in range(2 * GROUP_BLOCKS):
                    chi[up * 4 + i, j] = tile[i * BLOCK:(i + 1) * BLOCK, j * BLOCK:(j + 1) * BLOCK]
            return c

        lax.fori_loop(0, 3, multiply, 0)

    mine = row_turns[pl.ds(pl.multiple_of(b * BLOCK, BLOCK), BLOCK), :]
    turns[...] = jnp.dot(mine, spread[...], preferred_element_type=jnp.float32)

    row_from = [perm_ref[s, row * GROUP_BLOCKS + b] - row * GROUP_BLOCKS for s in range(NS)]
    col_group = (col // 2) * GROUP_BLOCKS

    def column(c, carry):
        col_from = [perm_ref[s, col * COL_BLOCKS + c] - col_group for s in range(NS)]
        here = pl.ds(pl.multiple_of(c * BLOCK, BLOCK), BLOCK)

        for t in range(BLOCK // 8):
            rows = slice(t * 8, (t + 1) * 8)
            real = imag = None
            for s in range(NS):
                xr = chi[row_from[s], col_from[s], rows]
                xi = chi[row_from[s], col_from[s] + GROUP_BLOCKS, rows]
                cg = turns[rows, s * BLOCK:(s + 1) * BLOCK]
                sg = turns[rows, (NS + s) * BLOCK:(NS + s + 1) * BLOCK]
                ch, sh = col_cos[s, c], col_sin[s, c]
                turn_c = cg * ch + sg * sh
                turn_s = sg * ch - cg * sh
                add_r = turn_c * xr - turn_s * xi
                add_i = turn_c * xi + turn_s * xr
                real = add_r if s == 0 else real + add_r
                imag = add_i if s == 0 else imag + add_i
            out_ref[0, rows, here] = real
            out_ref[1, rows, here] = imag
        return carry

    lax.fori_loop(0, COL_BLOCKS, column, 0, unroll=2)


def symmetrize(block_perm, row_turns, col_turns, row_all, col_all, weights):
    vmem = pl.BlockSpec(memory_space=pltpu.VMEM)
    bf16, f32 = jnp.bfloat16, jnp.float32
    return pl.pallas_call(
        symmetrize_kernel,
        grid=(GROUP_BLOCKS,),
        out_shape=jax.ShapeDtypeStruct((2, GROUP, WIDE), f32),
        in_specs=[pl.BlockSpec(memory_space=pltpu.SMEM), vmem, vmem, vmem, vmem, vmem],
        out_specs=pl.BlockSpec((2, BLOCK, WIDE), lambda b: (0, b, 0)),
        scratch_shapes=[
            pltpu.VMEM((GROUP_BLOCKS, 2 * GROUP_BLOCKS, BLOCK, BLOCK), f32),
            pltpu.VMEM((GROUP, 2 * PAIRS), bf16),
            pltpu.VMEM((2 * PAIRS, 2 * GROUP), bf16),
            pltpu.VMEM((4 * NS, 2 * NS * BLOCK), bf16),
            pltpu.VMEM((BLOCK, 2 * NS * BLOCK), f32),
            pltpu.VMEM((NS, COL_BLOCKS, 8, BLOCK), f32),
            pltpu.VMEM((NS, COL_BLOCKS, 8, BLOCK), f32),
        ],
        compiler_params=pltpu.CompilerParams(vmem_limit_bytes=48 * 2**20),
    )(block_perm, row_turns, col_turns, row_all, col_all, weights)


def shards(densities, pair_weight, block_perm, phase_index):
    row_all, col_all, weights, row_turns, col_turns = gather(densities, pair_weight.reshape(1, SHARE), phase_index)
    return symmetrize(block_perm, row_turns, col_turns, row_all, col_all, weights)


def solution(mesh):
    return jax.shard_map(
        shards,
        mesh=mesh,
        in_specs=(P(None, "row", "col"), P("row"), P(), P()),
        out_specs=P(None, "row", "col"),
        check_vma=False,
    )
```

```python
import functools
import math

import jax
import jax.numpy as jnp
from jax import lax
from jax.experimental import pallas as pl
from jax.experimental.pallas import tpu as pltpu
from jax.sharding import PartitionSpec as P

BLOCK = 128
NS = 8
PAIRS = 256
SHARE = 32
WIDE = 768
GROUP = 1536
GROUP_BLOCKS = 12
COL_BLOCKS = 6
FAR_LAG = 2
GATHER_VMEM = 16 * 2**20
NORM = -1.0 / math.sqrt(NS * PAIRS)
HALF_ROOT = math.sqrt(0.5)
MESH = pl.DeviceIdType.MESH


def turn_parts(phase):
    odd = jnp.where(phase % 2 == 1, HALF_ROOT, 1.0)
    cos_sign = jnp.where(jnp.logical_or(phase < 2, phase == 7), 1.0, jnp.where(jnp.logical_and(phase > 2, phase < 6), -1.0, 0.0))
    sin_sign = jnp.where(jnp.logical_and(phase > 0, phase < 4), 1.0, jnp.where(phase > 4, -1.0, 0.0))
    return cos_sign * odd, sin_sign * odd


def gather_kernel(
    d_ref, w_ref, phase_ref, hop_ref, col_ref, wt_ref, row_turns, col_turns,
    w_own, c_recv, line_recv, far_recv, sib_recv, mate_recv, w_recv, bulk, sib_send, cross_send,
    mate_send, w_send, local,
):
    row = lax.axis_index("row")
    col = lax.axis_index("col")
    y, k = row // 2, row % 2
    x, z = col // 4, col % 4
    zp, q = z % 2, z // 2
    zo = z + 1 - 2 * zp
    zc = (z + 3 + 2 * zp) % 4

    def dev(xx, yy, zz, kk):
        return (2 * yy + kk, 4 * xx + zz)

    on_line = q == k
    is_root = x == y
    to_sib = dev(x, y, z, 1 - k)
    to_zo = dev(x, y, zo, k)
    to_cross = dev(x, y, zc, q)

    def rows_of(yy, kk):
        return pl.ds(pl.multiple_of((2 * yy + kk) * SHARE, SHARE), SHARE)

    def pair_of(yy):
        return pl.ds(pl.multiple_of(yy * 2 * SHARE, 2 * SHARE), 2 * SHARE)

    def cols_of(zz):
        return pl.ds(pl.multiple_of(zz * WIDE, WIDE), WIDE)

    get_w = pltpu.make_async_copy(w_ref, w_own, local.at[1])
    get_w.start()
    keep = pltpu.make_async_copy(d_ref, col_ref.at[:, rows_of(y, k), cols_of(zp)], local.at[0])
    keep.start()

    barrier = pltpu.get_barrier_semaphore()

    def greet(target):
        pl.semaphore_signal(barrier, inc=1, device_id=target, device_id_type=MESH)

    for step in range(1, 8):
        greet(((row + step) % 8, col))
    greet(to_zo)

    @pl.when(jnp.logical_not(is_root))
    def _():
        for yy in range(4):
            greet(dev(y, yy, z, k))

    @pl.when(jnp.logical_not(on_line))
    def _():
        greet(dev(x, y, zc, 0))
        greet(dev(x, y, zc, 1))

    pl.semaphore_wait(barrier, 12)

    def copy(src, dst, send, recv, target):
        return pltpu.make_async_remote_copy(
            src_ref=src, dst_ref=dst, send_sem=send, recv_sem=recv, device_id=target, device_id_type=MESH
        )

    def c_at(yy, zz):
        return col_ref.at[:, rows_of(yy, k), cols_of(zz)]

    def r_at(which, yy, zz):
        return hop_ref.at[which, :, rows_of(yy, k), cols_of(zz)]

    def c_copy(yy, zz, target, src=None):
        there = c_at(yy, zz)
        return copy(there if src is None else src, there, bulk.at[0], c_recv.at[2 * yy + zz], target)

    def spread_block(zz, src):
        for step in range(1, 4):
            target = dev((x + step) % 4, x, z, k)
            copy(src, r_at(q, y, zz), bulk.at[0], line_recv.at[2 * y + zz], target).start()
        for step in range(4):
            yy = (x + step) % 4

            @pl.when(yy != y)
            def _():
                c_copy(y, zz, dev(x, yy, z, k), src).start()

    c_copy(y, zp, to_zo, d_ref).start()
    spread_block(zp, d_ref)

    cosine, sine = turn_parts(phase_ref[:, pl.ds(pl.multiple_of(col * WIDE, BLOCK), WIDE)])
    col_turns[0] = cosine
    col_turns[1] = sine

    def row_block(b, carry):
        phases = phase_ref[:, pl.ds(pl.multiple_of(row * GROUP + b * BLOCK, BLOCK), BLOCK)]
        both = jnp.concatenate(turn_parts(phases), axis=0)
        coarse = both.astype(jnp.bfloat16).astype(jnp.float32)
        pieces = jnp.concatenate([coarse, both - coarse], axis=0).T.astype(jnp.bfloat16)
        row_turns[pl.ds(pl.multiple_of(b * BLOCK, BLOCK), BLOCK), :] = pieces
        return carry

    lax.fori_loop(0, GROUP_BLOCKS, row_block, 0)
    keep.wait()
    c_copy(y, 1 - zp, to_zo).wait_recv()
    spread_block(1 - zp, c_at(y, 1 - zp))

    def sib_c(yy, kk):
        there = col_ref.at[:, rows_of(yy, kk), :]
        return copy(there, there, sib_send.at[0], sib_recv.at[yy], to_sib)

    sib_c(y, k).start()

    get_w.wait()
    lanes = lax.broadcasted_iota(jnp.int32, (SHARE, SHARE), 1)
    subs = lax.broadcasted_iota(jnp.int32, (SHARE, SHARE), 0)
    spread = jnp.where(lanes == subs, jnp.broadcast_to(w_own[...].astype(jnp.float32), (SHARE, SHARE)), 0.0)
    w_col = jnp.sum(spread, axis=1, keepdims=True)

    def w_at(origin):
        return wt_ref.at[pl.ds(pl.multiple_of(origin * SHARE, SHARE), SHARE), :]

    w_at(row)[...] = jnp.broadcast_to(w_col, (SHARE, BLOCK)).astype(jnp.bfloat16)
    for step in range(1, 8):
        target = ((row + step) % 8, col)
        copy(w_at(row), w_at(row), w_send.at[0], w_recv.at[row], target).start()

    def cross(yy, zz, part, from_col):
        there = hop_ref.at[q, part, rows_of(yy, k), cols_of(zz)]
        src = col_ref.at[part, rows_of(yy, k), cols_of(zz)] if from_col else there
        return copy(src, there, cross_send.at[0], far_recv.at[2 * yy + zz], to_cross)

    def cross_start(yy, zz, from_col):
        @pl.when(zp == 1)
        def _():
            cross(yy, zz, 0, from_col).start()

        @pl.when(zp == 0)
        def _():
            cross(yy, zz, 1, from_col).start()

    def cross_both(yy, zz):
        return copy(c_at(yy, zz), r_at(q, yy, zz), cross_send.at[0], far_recv.at[2 * yy + zz], to_cross)

    def sib_r(yy, zz):
        return copy(r_at(q, yy, zz), r_at(q, yy, zz), sib_send.at[1], sib_recv.at[4], to_sib)

    def line(n):
        yy = (y + n % 4) % 4
        zz = zp if n < 4 else 1 - zp

        @pl.when(is_root)
        def _():
            if n % 4 != 0:
                c_copy(yy, zz, to_zo).wait_recv()
            if n % 4 == 2:
                cross_both(yy, zz).start()
            else:
                cross_start(yy, zz, True)
            if n > 4:
                sib_c(yy, k).start()

        @pl.when(jnp.logical_not(is_root))
        def _():
            copy(r_at(q, yy, zz), r_at(q, yy, zz), bulk.at[0], line_recv.at[2 * yy + zz], to_zo).wait_recv()
            cross_start(yy, zz, False)

            @pl.when(jnp.logical_not(on_line))
            def _():
                sib_r(yy, zz).start()

    def mate(yy, zz, part):
        there = hop_ref.at[k, part, pair_of(yy), cols_of(zz)]
        return copy(there, there, mate_send.at[0], mate_recv.at[0], to_zo)

    def far(n):
        yy = (y + n % 4) % 4
        zz = 1 - zp if n < 4 else zp

        def arrive(part):
            there = hop_ref.at[k, part, pair_of(yy), cols_of(zz)]
            copy(there, there, mate_send.at[0], far_recv.at[2 * yy + zz], to_zo).wait_recv()
            mate(yy, zz, part).start()

        relayed = jnp.logical_not(on_line)
        if n % 4 == 2:
            @pl.when(jnp.logical_and(relayed, is_root))
            def _():
                there = hop_ref.at[k, :, pair_of(yy), cols_of(zz)]
                copy(there, there, mate_send.at[0], far_recv.at[2 * yy + zz], to_zo).wait_recv()

            relayed = jnp.logical_and(relayed, jnp.logical_not(is_root))

        @pl.when(jnp.logical_and(relayed, zp == 0))
        def _():
            arrive(0)

        @pl.when(jnp.logical_and(relayed, zp == 1))
        def _():
            arrive(1)

    for step in range(8 + FAR_LAG):
        if step < 8:
            line(step)
        if step >= FAR_LAG:
            far(step - FAR_LAG)

    @pl.when(jnp.logical_not(is_root))
    def _():
        for step in range(1, 4):
            yy = (y + step) % 4
            c_copy(yy, 0, to_zo).wait_recv()
            c_copy(yy, 1, to_zo).wait_recv()
            sib_c(yy, k).start()

    for yy in range(4):
        sib_c(yy, 1 - k).wait_recv()

    half = hop_ref.at[k, :, 0:PAIRS // 2, :]
    whole = hop_ref.at[k, 0]
    most = hop_ref.at[k, 0, 0:3 * PAIRS // 4, :]
    far_root = jnp.logical_and(jnp.logical_not(on_line), is_root)
    far_other = jnp.logical_and(jnp.logical_not(on_line), jnp.logical_not(is_root))

    @pl.when(far_root)
    def _():
        copy(most, most, mate_send.at[0], mate_recv.at[0], to_zo).wait_recv()

    @pl.when(far_other)
    def _():
        copy(whole, whole, mate_send.at[0], mate_recv.at[0], to_zo).wait_recv()

    @pl.when(jnp.logical_and(on_line, jnp.logical_not(is_root)))
    def _():
        copy(half, half, sib_send.at[1], sib_recv.at[4], to_sib).wait_recv()

    @pl.when(jnp.logical_and(on_line, is_root))
    def _():
        hop_ref[k] = col_ref[...]

    for step in range(1, 8):
        origin = (row + step) % 8
        copy(w_at(origin), w_at(origin), w_send.at[0], w_recv.at[origin], to_sib).wait_recv()

    sent = col_ref.at[:, 0:208, :]
    copy(sent, sent, bulk.at[0], c_recv.at[0], to_zo).wait_send()
    copy(half, half, sib_send.at[0], sib_recv.at[0], to_sib).wait_send()
    part_half = hop_ref.at[k, 0, 0:PAIRS // 2, :]
    part_more = hop_ref.at[k, 0, 0:5 * PAIRS // 8, :]

    @pl.when(is_root)
    def _():
        copy(part_more, part_more, cross_send.at[0], far_recv.at[0], to_zo).wait_send()

    @pl.when(jnp.logical_not(is_root))
    def _():
        copy(part_half, part_half, cross_send.at[0], far_recv.at[0], to_zo).wait_send()

    w_sent = wt_ref.at[0:7 * SHARE, :]
    copy(w_sent, w_sent, w_send.at[0], w_recv.at[0], to_sib).wait_send()

    @pl.when(far_root)
    def _():
        copy(most, most, mate_send.at[0], mate_recv.at[0], to_zo).wait_send()

    @pl.when(far_other)
    def _():
        copy(whole, whole, mate_send.at[0], mate_recv.at[0], to_zo).wait_send()
        copy(half, half, sib_send.at[1], sib_recv.at[4], to_sib).wait_send()


def gather(densities, weights, phase_index):
    vmem = pl.BlockSpec(memory_space=pltpu.VMEM)
    hbm = pl.BlockSpec(memory_space=pltpu.HBM)
    dma = pltpu.SemaphoreType.DMA
    return pl.pallas_call(
        gather_kernel,
        out_shape=[
            jax.ShapeDtypeStruct((2, 2, PAIRS, GROUP), jnp.bfloat16),
            jax.ShapeDtypeStruct((2, PAIRS, GROUP), jnp.bfloat16),
            jax.ShapeDtypeStruct((PAIRS, BLOCK), jnp.bfloat16),
            jax.ShapeDtypeStruct((GROUP, 4 * NS), jnp.bfloat16),
            jax.ShapeDtypeStruct((2, NS, WIDE), jnp.float32),
        ],
        in_specs=[hbm, hbm, vmem],
        out_specs=[vmem, vmem, vmem, vmem, vmem],
        scratch_shapes=[
            pltpu.VMEM((1, SHARE), jnp.bfloat16),
            dma((8,)), dma((8,)), dma((8,)), dma((5,)), dma((1,)), dma((8,)), dma((1,)), dma((2,)), dma((1,)),
            dma((1,)), dma((1,)), dma((2,)),
        ],
        compiler_params=pltpu.CompilerParams(
            collective_id=0, has_side_effects=True, vmem_limit_bytes=GATHER_VMEM
        ),
    )(densities, weights, phase_index)


def symmetrize_kernel(
    perm_ref, row_turns, col_turns, hop_ref, col_ref, wt_ref, out_ref,
    chi, left, right, spread, turns, col_cos, col_sin,
):
    row = lax.axis_index("row")
    col = lax.axis_index("col")
    b = pl.program_id(0)

    @pl.when(b == 0)
    def _():
        entry = lax.broadcasted_iota(jnp.int32, (4 * NS, 2 * NS * BLOCK), 0) % (2 * NS)
        block = lax.broadcasted_iota(jnp.int32, (4 * NS, 2 * NS * BLOCK), 1) // BLOCK
        spread[...] = jnp.where(entry == block, 1.0, 0.0).astype(jnp.bfloat16)

        cosine, sine = col_turns[0], col_turns[1]
        for s in range(NS):
            for c in range(COL_BLOCKS):
                lane = slice(c * BLOCK, (c + 1) * BLOCK)
                col_cos[s, c] = jnp.broadcast_to(cosine[s:s + 1, lane], (8, BLOCK))
                col_sin[s, c] = jnp.broadcast_to(sine[s:s + 1, lane], (8, BLOCK))

        weight = wt_ref[...].astype(jnp.float32) * NORM

        def prepare_left(t, c):
            tile = pl.ds(pl.multiple_of(t * BLOCK, BLOCK), BLOCK)
            for part in range(2):
                scaled = hop_ref[row % 2, part, :, tile].astype(jnp.float32) * weight
                left[tile, part * PAIRS:(part + 1) * PAIRS] = scaled.T.astype(jnp.bfloat16)
            return c

        lax.fori_loop(0, GROUP_BLOCKS, prepare_left, 0, unroll=6)
        right[0:PAIRS, 0:GROUP] = col_ref[0]
        right[PAIRS:2 * PAIRS, 0:GROUP] = col_ref[1]
        right[0:PAIRS, GROUP:2 * GROUP] = -col_ref[1]
        right[PAIRS:2 * PAIRS, GROUP:2 * GROUP] = col_ref[0]

        def multiply(up, c):
            rows = pl.ds(pl.multiple_of(up * 768, 768), 768)
            tile = jnp.dot(left[rows, :], right[...], preferred_element_type=jnp.float32)
            for i in range(6):
                for j in range(2 * GROUP_BLOCKS):
                    chi[up * 6 + i, j] = tile[i * BLOCK:(i + 1) * BLOCK, j * BLOCK:(j + 1) * BLOCK]
            return c

        lax.fori_loop(0, 2, multiply, 0)

    mine = row_turns[pl.ds(pl.multiple_of(b * BLOCK, BLOCK), BLOCK), :]
    turns[...] = jnp.dot(mine, spread[...], preferred_element_type=jnp.float32)

    row_from = [perm_ref[s, row * GROUP_BLOCKS + b] - row * GROUP_BLOCKS for s in range(NS)]
    col_group = (col // 2) * GROUP_BLOCKS

    def column(c, carry):
        col_from = [perm_ref[s, col * COL_BLOCKS + c] - col_group for s in range(NS)]
        here = pl.ds(pl.multiple_of(c * BLOCK, BLOCK), BLOCK)

        for t in range(BLOCK // 8):
            rows = slice(t * 8, (t + 1) * 8)
            real = imag = None
            for s in range(NS):
                xr = chi[row_from[s], col_from[s], rows]
                xi = chi[row_from[s], col_from[s] + GROUP_BLOCKS, rows]
                cg = turns[rows, s * BLOCK:(s + 1) * BLOCK]
                sg = turns[rows, (NS + s) * BLOCK:(NS + s + 1) * BLOCK]
                ch, sh = col_cos[s, c], col_sin[s, c]
                turn_c = cg * ch + sg * sh
                turn_s = sg * ch - cg * sh
                add_r = turn_c * xr - turn_s * xi
                add_i = turn_c * xi + turn_s * xr
                real = add_r if s == 0 else real + add_r
                imag = add_i if s == 0 else imag + add_i
            out_ref[0, rows, here] = real
            out_ref[1, rows, here] = imag
        return carry

    lax.fori_loop(0, COL_BLOCKS, column, 0, unroll=2)


def symmetrize(block_perm, row_turns, col_turns, row_all, col_all, weights):
    vmem = pl.BlockSpec(memory_space=pltpu.VMEM)
    bf16, f32 = jnp.bfloat16, jnp.float32
    return pl.pallas_call(
        symmetrize_kernel,
        grid=(GROUP_BLOCKS,),
        out_shape=jax.ShapeDtypeStruct((2, GROUP, WIDE), f32),
        in_specs=[pl.BlockSpec(memory_space=pltpu.SMEM), vmem, vmem, vmem, vmem, vmem],
        out_specs=pl.BlockSpec((2, BLOCK, WIDE), lambda b: (0, b, 0)),
        scratch_shapes=[
            pltpu.VMEM((GROUP_BLOCKS, 2 * GROUP_BLOCKS, BLOCK, BLOCK), f32),
            pltpu.VMEM((GROUP, 2 * PAIRS), bf16),
            pltpu.VMEM((2 * PAIRS, 2 * GROUP), bf16),
            pltpu.VMEM((4 * NS, 2 * NS * BLOCK), bf16),
            pltpu.VMEM((BLOCK, 2 * NS * BLOCK), f32),
            pltpu.VMEM((NS, COL_BLOCKS, 8, BLOCK), f32),
            pltpu.VMEM((NS, COL_BLOCKS, 8, BLOCK), f32),
        ],
        compiler_params=pltpu.CompilerParams(vmem_limit_bytes=48 * 2**20),
    )(block_perm, row_turns, col_turns, row_all, col_all, weights)


def shards(densities, pair_weight, block_perm, phase_index):
    row_all, col_all, weights, row_turns, col_turns = gather(densities, pair_weight.reshape(1, SHARE), phase_index)
    return symmetrize(block_perm, row_turns, col_turns, row_all, col_all, weights)


def solution(mesh):
    return jax.shard_map(
        shards,
        mesh=mesh,
        in_specs=(P(None, "row", "col"), P("row"), P(), P()),
        out_specs=P(None, "row", "col"),
        check_vma=False,
    )
```

```python
import functools
import math

import jax
import jax.numpy as jnp
from jax import lax
from jax.experimental import pallas as pl
from jax.experimental.pallas import tpu as pltpu
from jax.sharding import PartitionSpec as P

BLOCK = 128
NS = 8
PAIRS = 256
SHARE = 32
WIDE = 768
GROUP = 1536
GROUP_BLOCKS = 12
COL_BLOCKS = 6
FAR_LAG = 3
GATHER_VMEM = 16 * 2**20
NORM = -1.0 / math.sqrt(NS * PAIRS)
HALF_ROOT = math.sqrt(0.5)
MESH = pl.DeviceIdType.MESH


def turn_parts(phase):
    odd = jnp.where(phase % 2 == 1, HALF_ROOT, 1.0)
    cos_sign = jnp.where(jnp.logical_or(phase < 2, phase == 7), 1.0, jnp.where(jnp.logical_and(phase > 2, phase < 6), -1.0, 0.0))
    sin_sign = jnp.where(jnp.logical_and(phase > 0, phase < 4), 1.0, jnp.where(phase > 4, -1.0, 0.0))
    return cos_sign * odd, sin_sign * odd


def gather_kernel(
    d_ref, w_ref, phase_ref, hop_ref, col_ref, wt_ref, row_turns, col_turns,
    w_own, c_recv, line_recv, far_recv, sib_recv, mate_recv, w_recv, bulk, sib_send, cross_send,
    mate_send, w_send, local,
):
    row = lax.axis_index("row")
    col = lax.axis_index("col")
    y, k = row // 2, row % 2
    x, z = col // 4, col % 4
    zp, q = z % 2, z // 2
    zo = z + 1 - 2 * zp
    zc = (z + 3 + 2 * zp) % 4

    def dev(xx, yy, zz, kk):
        return (2 * yy + kk, 4 * xx + zz)

    on_line = q == k
    is_root = x == y
    to_sib = dev(x, y, z, 1 - k)
    to_zo = dev(x, y, zo, k)
    to_cross = dev(x, y, zc, q)

    def rows_of(yy, kk):
        return pl.ds(pl.multiple_of((2 * yy + kk) * SHARE, SHARE), SHARE)

    def pair_of(yy):
        return pl.ds(pl.multiple_of(yy * 2 * SHARE, 2 * SHARE), 2 * SHARE)

    def cols_of(zz):
        return pl.ds(pl.multiple_of(zz * WIDE, WIDE), WIDE)

    get_w = pltpu.make_async_copy(w_ref, w_own, local.at[1])
    get_w.start()
    keep = pltpu.make_async_copy(d_ref, col_ref.at[:, rows_of(y, k), cols_of(zp)], local.at[0])
    keep.start()

    barrier = pltpu.get_barrier_semaphore()

    def greet(target):
        pl.semaphore_signal(barrier, inc=1, device_id=target, device_id_type=MESH)

    for step in range(1, 8):
        greet(((row + step) % 8, col))
    greet(to_zo)

    @pl.when(jnp.logical_not(is_root))
    def _():
        for yy in range(4):
            greet(dev(y, yy, z, k))

    @pl.when(jnp.logical_not(on_line))
    def _():
        greet(dev(x, y, zc, 0))
        greet(dev(x, y, zc, 1))

    pl.semaphore_wait(barrier, 12)

    def copy(src, dst, send, recv, target):
        return pltpu.make_async_remote_copy(
            src_ref=src, dst_ref=dst, send_sem=send, recv_sem=recv, device_id=target, device_id_type=MESH
        )

    def c_at(yy, zz):
        return col_ref.at[:, rows_of(yy, k), cols_of(zz)]

    def r_at(which, yy, zz):
        return hop_ref.at[which, :, rows_of(yy, k), cols_of(zz)]

    def c_copy(yy, zz, target, src=None):
        there = c_at(yy, zz)
        return copy(there if src is None else src, there, bulk.at[0], c_recv.at[2 * yy + zz], target)

    def spread_block(zz, src):
        for step in range(1, 4):
            target = dev((x + step) % 4, x, z, k)
            copy(src, r_at(q, y, zz), bulk.at[0], line_recv.at[2 * y + zz], target).start()
        for step in range(4):
            yy = (x + step) % 4

            @pl.when(yy != y)
            def _():
                c_copy(y, zz, dev(x, yy, z, k), src).start()

    c_copy(y, zp, to_zo, d_ref).start()
    spread_block(zp, d_ref)

    cosine, sine = turn_parts(phase_ref[:, pl.ds(pl.multiple_of(col * WIDE, BLOCK), WIDE)])
    col_turns[0] = cosine
    col_turns[1] = sine

    def row_block(b, carry):
        phases = phase_ref[:, pl.ds(pl.multiple_of(row * GROUP + b * BLOCK, BLOCK), BLOCK)]
        both = jnp.concatenate(turn_parts(phases), axis=0)
        coarse = both.astype(jnp.bfloat16).astype(jnp.float32)
        pieces = jnp.concatenate([coarse, both - coarse], axis=0).T.astype(jnp.bfloat16)
        row_turns[pl.ds(pl.multiple_of(b * BLOCK, BLOCK), BLOCK), :] = pieces
        return carry

    lax.fori_loop(0, GROUP_BLOCKS, row_block, 0)
    keep.wait()
    c_copy(y, 1 - zp, to_zo).wait_recv()
    spread_block(1 - zp, c_at(y, 1 - zp))

    def sib_c(yy, kk):
        there = col_ref.at[:, rows_of(yy, kk), :]
        return copy(there, there, sib_send.at[0], sib_recv.at[yy], to_sib)

    sib_c(y, k).start()

    get_w.wait()
    lanes = lax.broadcasted_iota(jnp.int32, (SHARE, SHARE), 1)
    subs = lax.broadcasted_iota(jnp.int32, (SHARE, SHARE), 0)
    spread = jnp.where(lanes == subs, jnp.broadcast_to(w_own[...].astype(jnp.float32), (SHARE, SHARE)), 0.0)
    w_col = jnp.sum(spread, axis=1, keepdims=True)

    def w_at(origin):
        return wt_ref.at[pl.ds(pl.multiple_of(origin * SHARE, SHARE), SHARE), :]

    w_at(row)[...] = jnp.broadcast_to(w_col, (SHARE, BLOCK)).astype(jnp.bfloat16)
    for step in range(1, 8):
        target = ((row + step) % 8, col)
        copy(w_at(row), w_at(row), w_send.at[0], w_recv.at[row], target).start()

    def cross(yy, zz, part, from_col):
        there = hop_ref.at[q, part, rows_of(yy, k), cols_of(zz)]
        src = col_ref.at[part, rows_of(yy, k), cols_of(zz)] if from_col else there
        return copy(src, there, cross_send.at[0], far_recv.at[2 * yy + zz], to_cross)

    def cross_start(yy, zz, from_col):
        @pl.when(zp == 1)
        def _():
            cross(yy, zz, 0, from_col).start()

        @pl.when(zp == 0)
        def _():
            cross(yy, zz, 1, from_col).start()

    def cross_both(yy, zz):
        return copy(c_at(yy, zz), r_at(q, yy, zz), cross_send.at[0], far_recv.at[2 * yy + zz], to_cross)

    def sib_r(yy, zz):
        return copy(r_at(q, yy, zz), r_at(q, yy, zz), sib_send.at[1], sib_recv.at[4], to_sib)

    def line(n):
        yy = (y + n % 4) % 4
        zz = zp if n < 4 else 1 - zp

        @pl.when(is_root)
        def _():
            if n % 4 != 0:
                c_copy(yy, zz, to_zo).wait_recv()
            if n % 4 == 2:
                cross_both(yy, zz).start()
            else:
                cross_start(yy, zz, True)
            if n > 4:
                sib_c(yy, k).start()

        @pl.when(jnp.logical_not(is_root))
        def _():
            copy(r_at(q, yy, zz), r_at(q, yy, zz), bulk.at[0], line_recv.at[2 * yy + zz], to_zo).wait_recv()
            cross_start(yy, zz, False)

            @pl.when(jnp.logical_not(on_line))
            def _():
                sib_r(yy, zz).start()

    def mate(yy, zz, part):
        there = hop_ref.at[k, part, pair_of(yy), cols_of(zz)]
        return copy(there, there, mate_send.at[0], mate_recv.at[0], to_zo)

    def far(n):
        yy = (y + n % 4) % 4
        zz = 1 - zp if n < 4 else zp

        def arrive(part):
            there = hop_ref.at[k, part, pair_of(yy), cols_of(zz)]
            copy(there, there, mate_send.at[0], far_recv.at[2 * yy + zz], to_zo).wait_recv()
            mate(yy, zz, part).start()

        relayed = jnp.logical_not(on_line)
        if n % 4 == 2:
            @pl.when(jnp.logical_and(relayed, is_root))
            def _():
                there = hop_ref.at[k, :, pair_of(yy), cols_of(zz)]
                copy(there, there, mate_send.at[0], far_recv.at[2 * yy + zz], to_zo).wait_recv()

            relayed = jnp.logical_and(relayed, jnp.logical_not(is_root))

        @pl.when(jnp.logical_and(relayed, zp == 0))
        def _():
            arrive(0)

        @pl.when(jnp.logical_and(relayed, zp == 1))
        def _():
            arrive(1)

    for step in range(8 + FAR_LAG):
        if step < 8:
            line(step)
        if step >= FAR_LAG:
            far(step - FAR_LAG)

    @pl.when(jnp.logical_not(is_root))
    def _():
        for step in range(1, 4):
            yy = (y + step) % 4
            c_copy(yy, 0, to_zo).wait_recv()
            c_copy(yy, 1, to_zo).wait_recv()
            sib_c(yy, k).start()

    for yy in range(4):
        sib_c(yy, 1 - k).wait_recv()

    half = hop_ref.at[k, :, 0:PAIRS // 2, :]
    whole = hop_ref.at[k, 0]
    most = hop_ref.at[k, 0, 0:3 * PAIRS // 4, :]
    far_root = jnp.logical_and(jnp.logical_not(on_line), is_root)
    far_other = jnp.logical_and(jnp.logical_not(on_line), jnp.logical_not(is_root))

    @pl.when(far_root)
    def _():
        copy(most, most, mate_send.at[0], mate_recv.at[0], to_zo).wait_recv()

    @pl.when(far_other)
    def _():
        copy(whole, whole, mate_send.at[0], mate_recv.at[0], to_zo).wait_recv()

    @pl.when(jnp.logical_and(on_line, jnp.logical_not(is_root)))
    def _():
        copy(half, half, sib_send.at[1], sib_recv.at[4], to_sib).wait_recv()

    @pl.when(jnp.logical_and(on_line, is_root))
    def _():
        hop_ref[k] = col_ref[...]

    for step in range(1, 8):
        origin = (row + step) % 8
        copy(w_at(origin), w_at(origin), w_send.at[0], w_recv.at[origin], to_sib).wait_recv()

    sent = col_ref.at[:, 0:208, :]
    copy(sent, sent, bulk.at[0], c_recv.at[0], to_zo).wait_send()
    copy(half, half, sib_send.at[0], sib_recv.at[0], to_sib).wait_send()
    part_half = hop_ref.at[k, 0, 0:PAIRS // 2, :]
    part_more = hop_ref.at[k, 0, 0:5 * PAIRS // 8, :]

    @pl.when(is_root)
    def _():
        copy(part_more, part_more, cross_send.at[0], far_recv.at[0], to_zo).wait_send()

    @pl.when(jnp.logical_not(is_root))
    def _():
        copy(part_half, part_half, cross_send.at[0], far_recv.at[0], to_zo).wait_send()

    w_sent = wt_ref.at[0:7 * SHARE, :]
    copy(w_sent, w_sent, w_send.at[0], w_recv.at[0], to_sib).wait_send()

    @pl.when(far_root)
    def _():
        copy(most, most, mate_send.at[0], mate_recv.at[0], to_zo).wait_send()

    @pl.when(far_other)
    def _():
        copy(whole, whole, mate_send.at[0], mate_recv.at[0], to_zo).wait_send()
        copy(half, half, sib_send.at[1], sib_recv.at[4], to_sib).wait_send()


def gather(densities, weights, phase_index):
    vmem = pl.BlockSpec(memory_space=pltpu.VMEM)
    hbm = pl.BlockSpec(memory_space=pltpu.HBM)
    dma = pltpu.SemaphoreType.DMA
    return pl.pallas_call(
        gather_kernel,
        out_shape=[
            jax.ShapeDtypeStruct((2, 2, PAIRS, GROUP), jnp.bfloat16),
            jax.ShapeDtypeStruct((2, PAIRS, GROUP), jnp.bfloat16),
            jax.ShapeDtypeStruct((PAIRS, BLOCK), jnp.bfloat16),
            jax.ShapeDtypeStruct((GROUP, 4 * NS), jnp.bfloat16),
            jax.ShapeDtypeStruct((2, NS, WIDE), jnp.float32),
        ],
        in_specs=[hbm, hbm, vmem],
        out_specs=[vmem, vmem, vmem, vmem, vmem],
        scratch_shapes=[
            pltpu.VMEM((1, SHARE), jnp.bfloat16),
            dma((8,)), dma((8,)), dma((8,)), dma((5,)), dma((1,)), dma((8,)), dma((1,)), dma((2,)), dma((1,)),
            dma((1,)), dma((1,)), dma((2,)),
        ],
        compiler_params=pltpu.CompilerParams(
            collective_id=0, has_side_effects=True, vmem_limit_bytes=GATHER_VMEM
        ),
    )(densities, weights, phase_index)


def symmetrize_kernel(
    perm_ref, row_turns, col_turns, hop_ref, col_ref, wt_ref, out_ref,
    chi, left, right, spread, turns, col_cos, col_sin,
):
    row = lax.axis_index("row")
    col = lax.axis_index("col")
    b = pl.program_id(0)

    @pl.when(b == 0)
    def _():
        entry = lax.broadcasted_iota(jnp.int32, (4 * NS, 2 * NS * BLOCK), 0) % (2 * NS)
        block = lax.broadcasted_iota(jnp.int32, (4 * NS, 2 * NS * BLOCK), 1) // BLOCK
        spread[...] = jnp.where(entry == block, 1.0, 0.0).astype(jnp.bfloat16)

        cosine, sine = col_turns[0], col_turns[1]
        for s in range(NS):
            for c in range(COL_BLOCKS):
                lane = slice(c * BLOCK, (c + 1) * BLOCK)
                col_cos[s, c] = jnp.broadcast_to(cosine[s:s + 1, lane], (8, BLOCK))
                col_sin[s, c] = jnp.broadcast_to(sine[s:s + 1, lane], (8, BLOCK))

        weight = wt_ref[...].astype(jnp.float32) * NORM

        def prepare_left(t, c):
            tile = pl.ds(pl.multiple_of(t * BLOCK, BLOCK), BLOCK)
            for part in range(2):
                scaled = hop_ref[row % 2, part, :, tile].astype(jnp.float32) * weight
                left[tile, part * PAIRS:(part + 1) * PAIRS] = scaled.T.astype(jnp.bfloat16)
            return c

        lax.fori_loop(0, GROUP_BLOCKS, prepare_left, 0, unroll=6)
        right[0:PAIRS, 0:GROUP] = col_ref[0]
        right[PAIRS:2 * PAIRS, 0:GROUP] = col_ref[1]
        right[0:PAIRS, GROUP:2 * GROUP] = -col_ref[1]
        right[PAIRS:2 * PAIRS, GROUP:2 * GROUP] = col_ref[0]

        def multiply(up, c):
            rows = pl.ds(pl.multiple_of(up * 768, 768), 768)
            tile = jnp.dot(left[rows, :], right[...], preferred_element_type=jnp.float32)
            for i in range(6):
                for j in range(2 * GROUP_BLOCKS):
                    chi[up * 6 + i, j] = tile[i * BLOCK:(i + 1) * BLOCK, j * BLOCK:(j + 1) * BLOCK]
            return c

        lax.fori_loop(0, 2, multiply, 0)

    mine = row_turns[pl.ds(pl.multiple_of(b * BLOCK, BLOCK), BLOCK), :]
    turns[...] = jnp.dot(mine, spread[...], preferred_element_type=jnp.float32)

    row_from = [perm_ref[s, row * GROUP_BLOCKS + b] - row * GROUP_BLOCKS for s in range(NS)]
    col_group = (col // 2) * GROUP_BLOCKS

    def column(c, carry):
        col_from = [perm_ref[s, col * COL_BLOCKS + c] - col_group for s in range(NS)]
        here = pl.ds(pl.multiple_of(c * BLOCK, BLOCK), BLOCK)

        for t in range(BLOCK // 8):
            rows = slice(t * 8, (t + 1) * 8)
            real = imag = None
            for s in range(NS):
                xr = chi[row_from[s], col_from[s], rows]
                xi = chi[row_from[s], col_from[s] + GROUP_BLOCKS, rows]
                cg = turns[rows, s * BLOCK:(s + 1) * BLOCK]
                sg = turns[rows, (NS + s) * BLOCK:(NS + s + 1) * BLOCK]
                ch, sh = col_cos[s, c], col_sin[s, c]
                turn_c = cg * ch + sg * sh
                turn_s = sg * ch - cg * sh
                add_r = turn_c * xr - turn_s * xi
                add_i = turn_c * xi + turn_s * xr
                real = add_r if s == 0 else real + add_r
                imag = add_i if s == 0 else imag + add_i
            out_ref[0, rows, here] = real
            out_ref[1, rows, here] = imag
        return carry

    lax.fori_loop(0, COL_BLOCKS, column, 0, unroll=2)


def symmetrize(block_perm, row_turns, col_turns, row_all, col_all, weights):
    vmem = pl.BlockSpec(memory_space=pltpu.VMEM)
    bf16, f32 = jnp.bfloat16, jnp.float32
    return pl.pallas_call(
        symmetrize_kernel,
        grid=(GROUP_BLOCKS,),
        out_shape=jax.ShapeDtypeStruct((2, GROUP, WIDE), f32),
        in_specs=[pl.BlockSpec(memory_space=pltpu.SMEM), vmem, vmem, vmem, vmem, vmem],
        out_specs=pl.BlockSpec((2, BLOCK, WIDE), lambda b: (0, b, 0)),
        scratch_shapes=[
            pltpu.VMEM((GROUP_BLOCKS, 2 * GROUP_BLOCKS, BLOCK, BLOCK), f32),
            pltpu.VMEM((GROUP, 2 * PAIRS), bf16),
            pltpu.VMEM((2 * PAIRS, 2 * GROUP), bf16),
            pltpu.VMEM((4 * NS, 2 * NS * BLOCK), bf16),
            pltpu.VMEM((BLOCK, 2 * NS * BLOCK), f32),
            pltpu.VMEM((NS, COL_BLOCKS, 8, BLOCK), f32),
            pltpu.VMEM((NS, COL_BLOCKS, 8, BLOCK), f32),
        ],
        compiler_params=pltpu.CompilerParams(vmem_limit_bytes=48 * 2**20),
    )(block_perm, row_turns, col_turns, row_all, col_all, weights)


def shards(densities, pair_weight, block_perm, phase_index):
    row_all, col_all, weights, row_turns, col_turns = gather(densities, pair_weight.reshape(1, SHARE), phase_index)
    return symmetrize(block_perm, row_turns, col_turns, row_all, col_all, weights)


def solution(mesh):
    return jax.shard_map(
        shards,
        mesh=mesh,
        in_specs=(P(None, "row", "col"), P("row"), P(), P()),
        out_specs=P(None, "row", "col"),
        check_vma=False,
    )
```

```python
import functools
import math

import jax
import jax.numpy as jnp
from jax import lax
from jax.experimental import pallas as pl
from jax.experimental.pallas import tpu as pltpu
from jax.sharding import PartitionSpec as P

BLOCK = 128
NS = 8
PAIRS = 256
SHARE = 32
WIDE = 768
GROUP = 1536
GROUP_BLOCKS = 12
COL_BLOCKS = 6
FAR_LAG = 3
GATHER_VMEM = 16 * 2**20
NORM = -1.0 / math.sqrt(NS * PAIRS)
HALF_ROOT = math.sqrt(0.5)
MESH = pl.DeviceIdType.MESH


def turn_parts(phase):
    odd = jnp.where(phase % 2 == 1, HALF_ROOT, 1.0)
    cos_sign = jnp.where(jnp.logical_or(phase < 2, phase == 7), 1.0, jnp.where(jnp.logical_and(phase > 2, phase < 6), -1.0, 0.0))
    sin_sign = jnp.where(jnp.logical_and(phase > 0, phase < 4), 1.0, jnp.where(phase > 4, -1.0, 0.0))
    return cos_sign * odd, sin_sign * odd


def gather_kernel(
    d_ref, w_ref, phase_ref, hop_ref, col_ref, wt_ref, row_turns, col_turns,
    w_own, c_recv, line_recv, far_recv, sib_recv, mate_recv, w_recv, bulk, sib_send, cross_send,
    mate_send, w_send, local,
):
    row = lax.axis_index("row")
    col = lax.axis_index("col")
    y, k = row // 2, row % 2
    x, z = col // 4, col % 4
    zp, q = z % 2, z // 2
    zo = z + 1 - 2 * zp
    zc = (z + 3 + 2 * zp) % 4

    def dev(xx, yy, zz, kk):
        return (2 * yy + kk, 4 * xx + zz)

    on_line = q == k
    is_root = x == y
    to_sib = dev(x, y, z, 1 - k)
    to_zo = dev(x, y, zo, k)
    to_cross = dev(x, y, zc, q)

    def rows_of(yy, kk):
        return pl.ds(pl.multiple_of((2 * yy + kk) * SHARE, SHARE), SHARE)

    def pair_of(yy):
        return pl.ds(pl.multiple_of(yy * 2 * SHARE, 2 * SHARE), 2 * SHARE)

    def cols_of(zz):
        return pl.ds(pl.multiple_of(zz * WIDE, WIDE), WIDE)

    get_w = pltpu.make_async_copy(w_ref, w_own, local.at[1])
    get_w.start()
    keep = pltpu.make_async_copy(d_ref, col_ref.at[:, rows_of(y, k), cols_of(zp)], local.at[0])
    keep.start()

    barrier = pltpu.get_barrier_semaphore()

    def greet(target):
        pl.semaphore_signal(barrier, inc=1, device_id=target, device_id_type=MESH)

    for step in range(1, 8):
        greet(((row + step) % 8, col))
    greet(to_zo)

    @pl.when(jnp.logical_not(is_root))
    def _():
        for yy in range(4):
            greet(dev(y, yy, z, k))

    @pl.when(jnp.logical_not(on_line))
    def _():
        greet(dev(x, y, zc, 0))
        greet(dev(x, y, zc, 1))

    pl.semaphore_wait(barrier, 12)

    def copy(src, dst, send, recv, target):
        return pltpu.make_async_remote_copy(
            src_ref=src, dst_ref=dst, send_sem=send, recv_sem=recv, device_id=target, device_id_type=MESH
        )

    def c_at(yy, zz):
        return col_ref.at[:, rows_of(yy, k), cols_of(zz)]

    def r_at(which, yy, zz):
        return hop_ref.at[which, :, rows_of(yy, k), cols_of(zz)]

    def c_copy(yy, zz, target, src=None):
        there = c_at(yy, zz)
        return copy(there if src is None else src, there, bulk.at[0], c_recv.at[2 * yy + zz], target)

    def spread_block(zz, src):
        for step in range(1, 4):
            target = dev((x + step) % 4, x, z, k)
            copy(src, r_at(q, y, zz), bulk.at[0], line_recv.at[2 * y + zz], target).start()
        for step in range(4):
            yy = (x + step) % 4

            @pl.when(yy != y)
            def _():
                c_copy(y, zz, dev(x, yy, z, k), src).start()

    c_copy(y, zp, to_zo, d_ref).start()
    spread_block(zp, d_ref)

    cosine, sine = turn_parts(phase_ref[:, pl.ds(pl.multiple_of(col * WIDE, BLOCK), WIDE)])
    col_turns[0] = cosine
    col_turns[1] = sine

    def row_block(b, carry):
        phases = phase_ref[:, pl.ds(pl.multiple_of(row * GROUP + b * BLOCK, BLOCK), BLOCK)]
        both = jnp.concatenate(turn_parts(phases), axis=0)
        coarse = both.astype(jnp.bfloat16).astype(jnp.float32)
        pieces = jnp.concatenate([coarse, both - coarse], axis=0).T.astype(jnp.bfloat16)
        row_turns[pl.ds(pl.multiple_of(b * BLOCK, BLOCK), BLOCK), :] = pieces
        return carry

    lax.fori_loop(0, GROUP_BLOCKS, row_block, 0)
    keep.wait()
    c_copy(y, 1 - zp, to_zo).wait_recv()
    spread_block(1 - zp, c_at(y, 1 - zp))

    def sib_c(yy, kk):
        there = col_ref.at[:, rows_of(yy, kk), :]
        return copy(there, there, sib_send.at[0], sib_recv.at[yy], to_sib)

    sib_c(y, k).start()

    get_w.wait()
    lanes = lax.broadcasted_iota(jnp.int32, (SHARE, SHARE), 1)
    subs = lax.broadcasted_iota(jnp.int32, (SHARE, SHARE), 0)
    spread = jnp.where(lanes == subs, jnp.broadcast_to(w_own[...].astype(jnp.float32), (SHARE, SHARE)), 0.0)
    w_col = jnp.sum(spread, axis=1, keepdims=True)

    def w_at(origin):
        return wt_ref.at[pl.ds(pl.multiple_of(origin * SHARE, SHARE), SHARE), :]

    w_at(row)[...] = jnp.broadcast_to(w_col, (SHARE, BLOCK)).astype(jnp.bfloat16)
    for step in range(1, 8):
        target = ((row + step) % 8, col)
        copy(w_at(row), w_at(row), w_send.at[0], w_recv.at[row], target).start()

    def cross(yy, zz, part, from_col):
        there = hop_ref.at[q, part, rows_of(yy, k), cols_of(zz)]
        src = col_ref.at[part, rows_of(yy, k), cols_of(zz)] if from_col else there
        return copy(src, there, cross_send.at[0], far_recv.at[2 * yy + zz], to_cross)

    def cross_start(yy, zz, from_col):
        @pl.when(zp == 1)
        def _():
            cross(yy, zz, 0, from_col).start()

        @pl.when(zp == 0)
        def _():
            cross(yy, zz, 1, from_col).start()

    def cross_both(yy, zz, src):
        return copy(src, r_at(q, yy, zz), cross_send.at[0], far_recv.at[2 * yy + zz], to_cross)

    def sib_r(yy, zz):
        return copy(r_at(q, yy, zz), r_at(q, yy, zz), sib_send.at[1], sib_recv.at[4], to_sib)

    def line(n):
        yy = (y + n % 4) % 4
        zz = zp if n < 4 else 1 - zp

        @pl.when(is_root)
        def _():
            if n % 4 != 0:
                c_copy(yy, zz, to_zo).wait_recv()
            if n % 4 == 2:
                cross_both(yy, zz, c_at(yy, zz)).start()
            else:
                cross_start(yy, zz, True)
            if n > 4:
                sib_c(yy, k).start()

        @pl.when(jnp.logical_not(is_root))
        def _():
            copy(r_at(q, yy, zz), r_at(q, yy, zz), bulk.at[0], line_recv.at[2 * yy + zz], to_zo).wait_recv()
            if n % 4 == 2:
                cross_both(yy, zz, r_at(q, yy, zz)).start()
            else:
                cross_start(yy, zz, False)

            @pl.when(jnp.logical_not(on_line))
            def _():
                sib_r(yy, zz).start()

    def mate(yy, zz, part):
        there = hop_ref.at[k, part, pair_of(yy), cols_of(zz)]
        return copy(there, there, mate_send.at[0], mate_recv.at[0], to_zo)

    def far(n):
        yy = (y + n % 4) % 4
        zz = 1 - zp if n < 4 else zp

        def arrive(part):
            there = hop_ref.at[k, part, pair_of(yy), cols_of(zz)]
            copy(there, there, mate_send.at[0], far_recv.at[2 * yy + zz], to_zo).wait_recv()
            mate(yy, zz, part).start()

        relayed = jnp.logical_not(on_line)
        if n % 4 == 2:
            @pl.when(relayed)
            def _():
                there = hop_ref.at[k, :, pair_of(yy), cols_of(zz)]
                copy(there, there, mate_send.at[0], far_recv.at[2 * yy + zz], to_zo).wait_recv()

            return

        @pl.when(jnp.logical_and(relayed, zp == 0))
        def _():
            arrive(0)

        @pl.when(jnp.logical_and(relayed, zp == 1))
        def _():
            arrive(1)

    for step in range(8 + FAR_LAG):
        if step < 8:
            line(step)
        if step >= FAR_LAG:
            far(step - FAR_LAG)

    @pl.when(jnp.logical_not(is_root))
    def _():
        for step in range(1, 4):
            yy = (y + step) % 4
            c_copy(yy, 0, to_zo).wait_recv()
            c_copy(yy, 1, to_zo).wait_recv()
            sib_c(yy, k).start()

    for yy in range(4):
        sib_c(yy, 1 - k).wait_recv()

    half = hop_ref.at[k, :, 0:PAIRS // 2, :]
    most = hop_ref.at[k, 0, 0:3 * PAIRS // 4, :]
    far_root = jnp.logical_and(jnp.logical_not(on_line), is_root)
    far_other = jnp.logical_and(jnp.logical_not(on_line), jnp.logical_not(is_root))

    @pl.when(far_root)
    def _():
        copy(most, most, mate_send.at[0], mate_recv.at[0], to_zo).wait_recv()

    @pl.when(far_other)
    def _():
        copy(most, most, mate_send.at[0], mate_recv.at[0], to_zo).wait_recv()

    @pl.when(jnp.logical_and(on_line, jnp.logical_not(is_root)))
    def _():
        copy(half, half, sib_send.at[1], sib_recv.at[4], to_sib).wait_recv()

    @pl.when(jnp.logical_and(on_line, is_root))
    def _():
        hop_ref[k] = col_ref[...]

    for step in range(1, 8):
        origin = (row + step) % 8
        copy(w_at(origin), w_at(origin), w_send.at[0], w_recv.at[origin], to_sib).wait_recv()

    sent = col_ref.at[:, 0:208, :]
    copy(sent, sent, bulk.at[0], c_recv.at[0], to_zo).wait_send()
    copy(half, half, sib_send.at[0], sib_recv.at[0], to_sib).wait_send()
    part_more = hop_ref.at[k, 0, 0:5 * PAIRS // 8, :]

    @pl.when(is_root)
    def _():
        copy(part_more, part_more, cross_send.at[0], far_recv.at[0], to_zo).wait_send()

    @pl.when(jnp.logical_not(is_root))
    def _():
        copy(part_more, part_more, cross_send.at[0], far_recv.at[0], to_zo).wait_send()

    w_sent = wt_ref.at[0:7 * SHARE, :]
    copy(w_sent, w_sent, w_send.at[0], w_recv.at[0], to_sib).wait_send()

    @pl.when(far_root)
    def _():
        copy(most, most, mate_send.at[0], mate_recv.at[0], to_zo).wait_send()

    @pl.when(far_other)
    def _():
        copy(most, most, mate_send.at[0], mate_recv.at[0], to_zo).wait_send()
        copy(half, half, sib_send.at[1], sib_recv.at[4], to_sib).wait_send()


def gather(densities, weights, phase_index):
    vmem = pl.BlockSpec(memory_space=pltpu.VMEM)
    hbm = pl.BlockSpec(memory_space=pltpu.HBM)
    dma = pltpu.SemaphoreType.DMA
    return pl.pallas_call(
        gather_kernel,
        out_shape=[
            jax.ShapeDtypeStruct((2, 2, PAIRS, GROUP), jnp.bfloat16),
            jax.ShapeDtypeStruct((2, PAIRS, GROUP), jnp.bfloat16),
            jax.ShapeDtypeStruct((PAIRS, BLOCK), jnp.bfloat16),
            jax.ShapeDtypeStruct((GROUP, 4 * NS), jnp.bfloat16),
            jax.ShapeDtypeStruct((2, NS, WIDE), jnp.float32),
        ],
        in_specs=[hbm, hbm, vmem],
        out_specs=[vmem, vmem, vmem, vmem, vmem],
        scratch_shapes=[
            pltpu.VMEM((1, SHARE), jnp.bfloat16),
            dma((8,)), dma((8,)), dma((8,)), dma((5,)), dma((1,)), dma((8,)), dma((1,)), dma((2,)), dma((1,)),
            dma((1,)), dma((1,)), dma((2,)),
        ],
        compiler_params=pltpu.CompilerParams(
            collective_id=0, has_side_effects=True, vmem_limit_bytes=GATHER_VMEM
        ),
    )(densities, weights, phase_index)


def symmetrize_kernel(
    perm_ref, row_turns, col_turns, hop_ref, col_ref, wt_ref, out_ref,
    chi, left, spread, turns, col_cos, col_sin,
):
    row = lax.axis_index("row")
    col = lax.axis_index("col")
    b = pl.program_id(0)

    @pl.when(b == 0)
    def _():
        entry = lax.broadcasted_iota(jnp.int32, (4 * NS, 2 * NS * BLOCK), 0) % (2 * NS)
        block = lax.broadcasted_iota(jnp.int32, (4 * NS, 2 * NS * BLOCK), 1) // BLOCK
        spread[...] = jnp.where(entry == block, 1.0, 0.0).astype(jnp.bfloat16)

        cosine, sine = col_turns[0], col_turns[1]
        for s in range(NS):
            for c in range(COL_BLOCKS):
                lane = slice(c * BLOCK, (c + 1) * BLOCK)
                col_cos[s, c] = jnp.broadcast_to(cosine[s:s + 1, lane], (8, BLOCK))
                col_sin[s, c] = jnp.broadcast_to(sine[s:s + 1, lane], (8, BLOCK))

        weight = wt_ref[...].astype(jnp.float32) * NORM

        def prepare_left(t, c):
            tile = pl.ds(pl.multiple_of(t * BLOCK, BLOCK), BLOCK)
            for part in range(2):
                scaled = hop_ref[row % 2, part, :, tile].astype(jnp.float32) * weight
                turned = scaled.astype(jnp.bfloat16).T
                left[tile, part * PAIRS:(part + 1) * PAIRS] = turned
                if part == 0:
                    left[tile, 2 * PAIRS:3 * PAIRS] = -turned
            return c

        lax.fori_loop(0, GROUP_BLOCKS, prepare_left, 0, unroll=12)
        right = col_ref[...].reshape(2 * PAIRS, GROUP)

        def multiply(up, c):
            rows = pl.ds(pl.multiple_of(up * 768, 768), 768)
            for part in range(2):
                pieces = left[rows, part * PAIRS:(part + 2) * PAIRS]
                tile = jnp.dot(pieces, right, preferred_element_type=jnp.float32)
                for i in range(6):
                    for j in range(GROUP_BLOCKS):
                        chi[up * 6 + i, part * GROUP_BLOCKS + j] = tile[i * BLOCK:(i + 1) * BLOCK, j * BLOCK:(j + 1) * BLOCK]
            return c

        lax.fori_loop(0, 2, multiply, 0)

    mine = row_turns[pl.ds(pl.multiple_of(b * BLOCK, BLOCK), BLOCK), :]
    turns[...] = jnp.dot(mine, spread[...], preferred_element_type=jnp.float32)

    row_from = [perm_ref[s, row * GROUP_BLOCKS + b] - row * GROUP_BLOCKS for s in range(NS)]
    col_group = (col // 2) * GROUP_BLOCKS

    def column(c, carry):
        col_from = [perm_ref[s, col * COL_BLOCKS + c] - col_group for s in range(NS)]
        here = pl.ds(pl.multiple_of(c * BLOCK, BLOCK), BLOCK)

        for t in range(BLOCK // 8):
            rows = slice(t * 8, (t + 1) * 8)
            real = imag = None
            for s in range(NS):
                xr = chi[row_from[s], col_from[s], rows]
                xi = chi[row_from[s], col_from[s] + GROUP_BLOCKS, rows]
                cg = turns[rows, s * BLOCK:(s + 1) * BLOCK]
                sg = turns[rows, (NS + s) * BLOCK:(NS + s + 1) * BLOCK]
                ch, sh = col_cos[s, c], col_sin[s, c]
                turn_c = cg * ch + sg * sh
                turn_s = sg * ch - cg * sh
                add_r = turn_c * xr - turn_s * xi
                add_i = turn_c * xi + turn_s * xr
                real = add_r if s == 0 else real + add_r
                imag = add_i if s == 0 else imag + add_i
            out_ref[0, rows, here] = real
            out_ref[1, rows, here] = imag
        return carry

    lax.fori_loop(0, COL_BLOCKS, column, 0, unroll=2)


def symmetrize(block_perm, row_turns, col_turns, row_all, col_all, weights):
    vmem = pl.BlockSpec(memory_space=pltpu.VMEM)
    bf16, f32 = jnp.bfloat16, jnp.float32
    return pl.pallas_call(
        symmetrize_kernel,
        grid=(GROUP_BLOCKS,),
        out_shape=jax.ShapeDtypeStruct((2, GROUP, WIDE), f32),
        in_specs=[pl.BlockSpec(memory_space=pltpu.SMEM), vmem, vmem, vmem, vmem, vmem],
        out_specs=pl.BlockSpec((2, BLOCK, WIDE), lambda b: (0, b, 0)),
        scratch_shapes=[
            pltpu.VMEM((GROUP_BLOCKS, 2 * GROUP_BLOCKS, BLOCK, BLOCK), f32),
            pltpu.VMEM((GROUP, 3 * PAIRS), bf16),
            pltpu.VMEM((4 * NS, 2 * NS * BLOCK), bf16),
            pltpu.VMEM((BLOCK, 2 * NS * BLOCK), f32),
            pltpu.VMEM((NS, COL_BLOCKS, 8, BLOCK), f32),
            pltpu.VMEM((NS, COL_BLOCKS, 8, BLOCK), f32),
        ],
        compiler_params=pltpu.CompilerParams(vmem_limit_bytes=48 * 2**20),
    )(block_perm, row_turns, col_turns, row_all, col_all, weights)


def shards(densities, pair_weight, block_perm, phase_index):
    row_all, col_all, weights, row_turns, col_turns = gather(densities, pair_weight.reshape(1, SHARE), phase_index)
    return symmetrize(block_perm, row_turns, col_turns, row_all, col_all, weights)


def solution(mesh):
    return jax.shard_map(
        shards,
        mesh=mesh,
        in_specs=(P(None, "row", "col"), P("row"), P(), P()),
        out_specs=P(None, "row", "col"),
        check_vma=False,
    )
```

```python
import functools
import math

import jax
import jax.numpy as jnp
from jax import lax
from jax.experimental import pallas as pl
from jax.experimental.pallas import tpu as pltpu
from jax.sharding import PartitionSpec as P

BLOCK = 128
NS = 8
PAIRS = 256
SHARE = 32
WIDE = 768
GROUP = 1536
GROUP_BLOCKS = 12
COL_BLOCKS = 6
FAR_LAG = 3
GATHER_VMEM = 16 * 2**20
NORM = -1.0 / math.sqrt(NS * PAIRS)
HALF_ROOT = math.sqrt(0.5)
MESH = pl.DeviceIdType.MESH


def turn_parts(phase):
    odd = jnp.where(phase % 2 == 1, HALF_ROOT, 1.0)
    cos_sign = jnp.where(jnp.logical_or(phase < 2, phase == 7), 1.0, jnp.where(jnp.logical_and(phase > 2, phase < 6), -1.0, 0.0))
    sin_sign = jnp.where(jnp.logical_and(phase > 0, phase < 4), 1.0, jnp.where(phase > 4, -1.0, 0.0))
    return cos_sign * odd, sin_sign * odd


def gather_kernel(
    d_ref, w_ref, phase_ref, hop_ref, col_ref, wt_ref, row_turns, col_turns,
    w_own, c_recv, line_recv, far_recv, sib_recv, mate_recv, w_recv, bulk, sib_send, cross_send,
    mate_send, w_send, local,
):
    row = lax.axis_index("row")
    col = lax.axis_index("col")
    y, k = row // 2, row % 2
    x, z = col // 4, col % 4
    zp, q = z % 2, z // 2
    zo = z + 1 - 2 * zp
    zc = (z + 3 + 2 * zp) % 4

    def dev(xx, yy, zz, kk):
        return (2 * yy + kk, 4 * xx + zz)

    on_line = q == k
    is_root = x == y
    to_sib = dev(x, y, z, 1 - k)
    to_zo = dev(x, y, zo, k)
    to_cross = dev(x, y, zc, q)

    def rows_of(yy, kk):
        return pl.ds(pl.multiple_of((2 * yy + kk) * SHARE, SHARE), SHARE)

    def pair_of(yy):
        return pl.ds(pl.multiple_of(yy * 2 * SHARE, 2 * SHARE), 2 * SHARE)

    def cols_of(zz):
        return pl.ds(pl.multiple_of(zz * WIDE, WIDE), WIDE)

    get_w = pltpu.make_async_copy(w_ref, w_own, local.at[1])
    get_w.start()
    keep = pltpu.make_async_copy(d_ref, col_ref.at[:, rows_of(y, k), cols_of(zp)], local.at[0])
    keep.start()

    barrier = pltpu.get_barrier_semaphore()

    def greet(target):
        pl.semaphore_signal(barrier, inc=1, device_id=target, device_id_type=MESH)

    for step in range(1, 8):
        greet(((row + step) % 8, col))
    greet(to_zo)

    @pl.when(jnp.logical_not(is_root))
    def _():
        for yy in range(4):
            greet(dev(y, yy, z, k))

    @pl.when(jnp.logical_not(on_line))
    def _():
        greet(dev(x, y, zc, 0))
        greet(dev(x, y, zc, 1))

    pl.semaphore_wait(barrier, 12)

    def copy(src, dst, send, recv, target):
        return pltpu.make_async_remote_copy(
            src_ref=src, dst_ref=dst, send_sem=send, recv_sem=recv, device_id=target, device_id_type=MESH
        )

    def c_at(yy, zz):
        return col_ref.at[:, rows_of(yy, k), cols_of(zz)]

    def r_at(which, yy, zz):
        return hop_ref.at[which, :, rows_of(yy, k), cols_of(zz)]

    def c_copy(yy, zz, target, src=None):
        there = c_at(yy, zz)
        return copy(there if src is None else src, there, bulk.at[0], c_recv.at[2 * yy + zz], target)

    def spread_block(zz, src):
        for step in range(1, 4):
            target = dev((x + step) % 4, x, z, k)
            copy(src, r_at(q, y, zz), bulk.at[0], line_recv.at[2 * y + zz], target).start()
        for step in range(4):
            yy = (x + step) % 4

            @pl.when(yy != y)
            def _():
                c_copy(y, zz, dev(x, yy, z, k), src).start()

    c_copy(y, zp, to_zo, d_ref).start()
    spread_block(zp, d_ref)

    keep.wait()
    c_copy(y, 1 - zp, to_zo).wait_recv()
    spread_block(1 - zp, c_at(y, 1 - zp))

    def sib_c(yy, kk):
        there = col_ref.at[:, rows_of(yy, kk), :]
        return copy(there, there, sib_send.at[0], sib_recv.at[yy], to_sib)

    sib_c(y, k).start()

    cosine, sine = turn_parts(phase_ref[:, pl.ds(pl.multiple_of(col * WIDE, BLOCK), WIDE)])
    col_turns[0] = cosine
    col_turns[1] = sine

    def row_block(b, carry):
        phases = phase_ref[:, pl.ds(pl.multiple_of(row * GROUP + b * BLOCK, BLOCK), BLOCK)]
        both = jnp.concatenate(turn_parts(phases), axis=0)
        coarse = both.astype(jnp.bfloat16).astype(jnp.float32)
        pieces = jnp.concatenate([coarse, both - coarse], axis=0).T.astype(jnp.bfloat16)
        row_turns[pl.ds(pl.multiple_of(b * BLOCK, BLOCK), BLOCK), :] = pieces
        return carry

    lax.fori_loop(0, GROUP_BLOCKS, row_block, 0)

    get_w.wait()
    lanes = lax.broadcasted_iota(jnp.int32, (SHARE, SHARE), 1)
    subs = lax.broadcasted_iota(jnp.int32, (SHARE, SHARE), 0)
    spread = jnp.where(lanes == subs, jnp.broadcast_to(w_own[...].astype(jnp.float32), (SHARE, SHARE)), 0.0)
    w_col = jnp.sum(spread, axis=1, keepdims=True)

    def w_at(origin):
        return wt_ref.at[pl.ds(pl.multiple_of(origin * SHARE, SHARE), SHARE), :]

    w_at(row)[...] = jnp.broadcast_to(w_col, (SHARE, BLOCK)).astype(jnp.bfloat16)
    for step in range(1, 8):
        target = ((row + step) % 8, col)
        copy(w_at(row), w_at(row), w_send.at[0], w_recv.at[row], target).start()

    def cross(yy, zz, part, from_col):
        there = hop_ref.at[q, part, rows_of(yy, k), cols_of(zz)]
        src = col_ref.at[part, rows_of(yy, k), cols_of(zz)] if from_col else there
        return copy(src, there, cross_send.at[0], far_recv.at[2 * yy + zz], to_cross)

    def cross_start(yy, zz, from_col):
        @pl.when(zp == 1)
        def _():
            cross(yy, zz, 0, from_col).start()

        @pl.when(zp == 0)
        def _():
            cross(yy, zz, 1, from_col).start()

    def cross_both(yy, zz, src):
        return copy(src, r_at(q, yy, zz), cross_send.at[0], far_recv.at[2 * yy + zz], to_cross)

    def sib_r(yy, zz):
        return copy(r_at(q, yy, zz), r_at(q, yy, zz), sib_send.at[1], sib_recv.at[4], to_sib)

    def line(n):
        yy = (y + n % 4) % 4
        zz = zp if n < 4 else 1 - zp

        @pl.when(is_root)
        def _():
            if n % 4 != 0:
                c_copy(yy, zz, to_zo).wait_recv()
            if n % 4 == 2:
                cross_both(yy, zz, c_at(yy, zz)).start()
            else:
                cross_start(yy, zz, True)
            if n > 4:
                sib_c(yy, k).start()

        @pl.when(jnp.logical_not(is_root))
        def _():
            copy(r_at(q, yy, zz), r_at(q, yy, zz), bulk.at[0], line_recv.at[2 * yy + zz], to_zo).wait_recv()
            if n % 4 == 2:
                cross_both(yy, zz, r_at(q, yy, zz)).start()
            else:
                cross_start(yy, zz, False)

            @pl.when(jnp.logical_not(on_line))
            def _():
                sib_r(yy, zz).start()

    def mate(yy, zz, part):
        there = hop_ref.at[k, part, pair_of(yy), cols_of(zz)]
        return copy(there, there, mate_send.at[0], mate_recv.at[0], to_zo)

    def far(n):
        yy = (y + n % 4) % 4
        zz = 1 - zp if n < 4 else zp

        def arrive(part):
            there = hop_ref.at[k, part, pair_of(yy), cols_of(zz)]
            copy(there, there, mate_send.at[0], far_recv.at[2 * yy + zz], to_zo).wait_recv()
            mate(yy, zz, part).start()

        relayed = jnp.logical_not(on_line)
        if n % 4 == 2:
            @pl.when(relayed)
            def _():
                there = hop_ref.at[k, :, pair_of(yy), cols_of(zz)]
                copy(there, there, mate_send.at[0], far_recv.at[2 * yy + zz], to_zo).wait_recv()

            return

        @pl.when(jnp.logical_and(relayed, zp == 0))
        def _():
            arrive(0)

        @pl.when(jnp.logical_and(relayed, zp == 1))
        def _():
            arrive(1)

    for step in range(8 + FAR_LAG):
        if step < 8:
            line(step)
        if step >= FAR_LAG:
            far(step - FAR_LAG)

    @pl.when(jnp.logical_not(is_root))
    def _():
        for step in range(1, 4):
            yy = (y + step) % 4
            c_copy(yy, 0, to_zo).wait_recv()
            c_copy(yy, 1, to_zo).wait_recv()
            sib_c(yy, k).start()

    for yy in range(4):
        sib_c(yy, 1 - k).wait_recv()

    half = hop_ref.at[k, :, 0:PAIRS // 2, :]
    most = hop_ref.at[k, 0, 0:3 * PAIRS // 4, :]
    far_root = jnp.logical_and(jnp.logical_not(on_line), is_root)
    far_other = jnp.logical_and(jnp.logical_not(on_line), jnp.logical_not(is_root))

    @pl.when(far_root)
    def _():
        copy(most, most, mate_send.at[0], mate_recv.at[0], to_zo).wait_recv()

    @pl.when(far_other)
    def _():
        copy(most, most, mate_send.at[0], mate_recv.at[0], to_zo).wait_recv()

    @pl.when(jnp.logical_and(on_line, jnp.logical_not(is_root)))
    def _():
        copy(half, half, sib_send.at[1], sib_recv.at[4], to_sib).wait_recv()

    @pl.when(jnp.logical_and(on_line, is_root))
    def _():
        hop_ref[k] = col_ref[...]

    for step in range(1, 8):
        origin = (row + step) % 8
        copy(w_at(origin), w_at(origin), w_send.at[0], w_recv.at[origin], to_sib).wait_recv()

    sent = col_ref.at[:, 0:208, :]
    copy(sent, sent, bulk.at[0], c_recv.at[0], to_zo).wait_send()
    copy(half, half, sib_send.at[0], sib_recv.at[0], to_sib).wait_send()
    part_more = hop_ref.at[k, 0, 0:5 * PAIRS // 8, :]

    @pl.when(is_root)
    def _():
        copy(part_more, part_more, cross_send.at[0], far_recv.at[0], to_zo).wait_send()

    @pl.when(jnp.logical_not(is_root))
    def _():
        copy(part_more, part_more, cross_send.at[0], far_recv.at[0], to_zo).wait_send()

    w_sent = wt_ref.at[0:7 * SHARE, :]
    copy(w_sent, w_sent, w_send.at[0], w_recv.at[0], to_sib).wait_send()

    @pl.when(far_root)
    def _():
        copy(most, most, mate_send.at[0], mate_recv.at[0], to_zo).wait_send()

    @pl.when(far_other)
    def _():
        copy(most, most, mate_send.at[0], mate_recv.at[0], to_zo).wait_send()
        copy(half, half, sib_send.at[1], sib_recv.at[4], to_sib).wait_send()


def gather(densities, weights, phase_index):
    vmem = pl.BlockSpec(memory_space=pltpu.VMEM)
    hbm = pl.BlockSpec(memory_space=pltpu.HBM)
    dma = pltpu.SemaphoreType.DMA
    return pl.pallas_call(
        gather_kernel,
        out_shape=[
            jax.ShapeDtypeStruct((2, 2, PAIRS, GROUP), jnp.bfloat16),
            jax.ShapeDtypeStruct((2, PAIRS, GROUP), jnp.bfloat16),
            jax.ShapeDtypeStruct((PAIRS, BLOCK), jnp.bfloat16),
            jax.ShapeDtypeStruct((GROUP, 4 * NS), jnp.bfloat16),
            jax.ShapeDtypeStruct((2, NS, WIDE), jnp.float32),
        ],
        in_specs=[hbm, hbm, vmem],
        out_specs=[vmem, vmem, vmem, vmem, vmem],
        scratch_shapes=[
            pltpu.VMEM((1, SHARE), jnp.bfloat16),
            dma((8,)), dma((8,)), dma((8,)), dma((5,)), dma((1,)), dma((8,)), dma((1,)), dma((2,)), dma((1,)),
            dma((1,)), dma((1,)), dma((2,)),
        ],
        compiler_params=pltpu.CompilerParams(
            collective_id=0, has_side_effects=True, vmem_limit_bytes=GATHER_VMEM
        ),
    )(densities, weights, phase_index)


def symmetrize_kernel(
    perm_ref, row_turns, col_turns, hop_ref, col_ref, wt_ref, out_ref,
    chi, left, spread, turns, col_cos, col_sin,
):
    row = lax.axis_index("row")
    col = lax.axis_index("col")
    b = pl.program_id(0)

    @pl.when(b == 0)
    def _():
        entry = lax.broadcasted_iota(jnp.int32, (4 * NS, 2 * NS * BLOCK), 0) % (2 * NS)
        block = lax.broadcasted_iota(jnp.int32, (4 * NS, 2 * NS * BLOCK), 1) // BLOCK
        spread[...] = jnp.where(entry == block, 1.0, 0.0).astype(jnp.bfloat16)

        cosine, sine = col_turns[0], col_turns[1]
        for s in range(NS):
            for c in range(COL_BLOCKS):
                lane = slice(c * BLOCK, (c + 1) * BLOCK)
                col_cos[s, c] = jnp.broadcast_to(cosine[s:s + 1, lane], (8, BLOCK))
                col_sin[s, c] = jnp.broadcast_to(sine[s:s + 1, lane], (8, BLOCK))

        weight = wt_ref[...].astype(jnp.float32) * NORM

        def prepare_left(t, c):
            tile = pl.ds(pl.multiple_of(t * BLOCK, BLOCK), BLOCK)
            for part in range(2):
                scaled = hop_ref[row % 2, part, :, tile].astype(jnp.float32) * weight
                turned = scaled.astype(jnp.bfloat16).T
                left[tile, part * PAIRS:(part + 1) * PAIRS] = turned
                if part == 0:
                    left[tile, 2 * PAIRS:3 * PAIRS] = -turned
            return c

        lax.fori_loop(0, GROUP_BLOCKS, prepare_left, 0, unroll=12)
        right = col_ref[...].reshape(2 * PAIRS, GROUP)

        def multiply(up, c):
            rows = pl.ds(pl.multiple_of(up * 768, 768), 768)
            for part in range(2):
                pieces = left[rows, part * PAIRS:(part + 2) * PAIRS]
                tile = jnp.dot(pieces, right, preferred_element_type=jnp.float32)
                for i in range(6):
                    for j in range(GROUP_BLOCKS):
                        chi[up * 6 + i, part * GROUP_BLOCKS + j] = tile[i * BLOCK:(i + 1) * BLOCK, j * BLOCK:(j + 1) * BLOCK]
            return c

        lax.fori_loop(0, 2, multiply, 0)

    mine = row_turns[pl.ds(pl.multiple_of(b * BLOCK, BLOCK), BLOCK), :]
    turns[...] = jnp.dot(mine, spread[...], preferred_element_type=jnp.float32)

    row_from = [perm_ref[s, row * GROUP_BLOCKS + b] - row * GROUP_BLOCKS for s in range(NS)]
    col_group = (col // 2) * GROUP_BLOCKS

    def column(c, carry):
        col_from = [perm_ref[s, col * COL_BLOCKS + c] - col_group for s in range(NS)]
        here = pl.ds(pl.multiple_of(c * BLOCK, BLOCK), BLOCK)

        for t in range(BLOCK // 8):
            rows = slice(t * 8, (t + 1) * 8)
            real = imag = None
            for s in range(NS):
                xr = chi[row_from[s], col_from[s], rows]
                xi = chi[row_from[s], col_from[s] + GROUP_BLOCKS, rows]
                cg = turns[rows, s * BLOCK:(s + 1) * BLOCK]
                sg = turns[rows, (NS + s) * BLOCK:(NS + s + 1) * BLOCK]
                ch, sh = col_cos[s, c], col_sin[s, c]
                turn_c = cg * ch + sg * sh
                turn_s = sg * ch - cg * sh
                add_r = turn_c * xr - turn_s * xi
                add_i = turn_c * xi + turn_s * xr
                real = add_r if s == 0 else real + add_r
                imag = add_i if s == 0 else imag + add_i
            out_ref[0, rows, here] = real
            out_ref[1, rows, here] = imag
        return carry

    lax.fori_loop(0, COL_BLOCKS, column, 0, unroll=2)


def symmetrize(block_perm, row_turns, col_turns, row_all, col_all, weights):
    vmem = pl.BlockSpec(memory_space=pltpu.VMEM)
    bf16, f32 = jnp.bfloat16, jnp.float32
    return pl.pallas_call(
        symmetrize_kernel,
        grid=(GROUP_BLOCKS,),
        out_shape=jax.ShapeDtypeStruct((2, GROUP, WIDE), f32),
        in_specs=[pl.BlockSpec(memory_space=pltpu.SMEM), vmem, vmem, vmem, vmem, vmem],
        out_specs=pl.BlockSpec((2, BLOCK, WIDE), lambda b: (0, b, 0)),
        scratch_shapes=[
            pltpu.VMEM((GROUP_BLOCKS, 2 * GROUP_BLOCKS, BLOCK, BLOCK), f32),
            pltpu.VMEM((GROUP, 3 * PAIRS), bf16),
            pltpu.VMEM((4 * NS, 2 * NS * BLOCK), bf16),
            pltpu.VMEM((BLOCK, 2 * NS * BLOCK), f32),
            pltpu.VMEM((NS, COL_BLOCKS, 8, BLOCK), f32),
            pltpu.VMEM((NS, COL_BLOCKS, 8, BLOCK), f32),
        ],
        compiler_params=pltpu.CompilerParams(vmem_limit_bytes=48 * 2**20),
    )(block_perm, row_turns, col_turns, row_all, col_all, weights)


def shards(densities, pair_weight, block_perm, phase_index):
    row_all, col_all, weights, row_turns, col_turns = gather(densities, pair_weight.reshape(1, SHARE), phase_index)
    return symmetrize(block_perm, row_turns, col_turns, row_all, col_all, weights)


def solution(mesh):
    return jax.shard_map(
        shards,
        mesh=mesh,
        in_specs=(P(None, "row", "col"), P("row"), P(), P()),
        out_specs=P(None, "row", "col"),
        check_vma=False,
    )
```
